128 devices in a mesh: row: 8 (over z_lo, y), col: 16 (over z_hi, x, core).
Axes of the slice: x: 4, y: 4, z: 4 (z_hi: 2, z_lo: 2; z = z_hi * 2 + z_lo), core: 2. Of those that a mesh axis runs over, the one named last changes fastest.
Arguments:
- features: bfloat16 [16, 6144, 128], P('col', 'row'), may hold values from -6 to 6
- tile_values: bfloat16 [8, 16, 96, 128, 128], P('row', 'col'), may hold values from -0.1875 to 0.1875
- tile_rows: int32 [8, 16, 96], P('row', 'col'), may hold values from 0 to 95
- tile_cols: int32 [8, 16, 96], P('row', 'col'), may hold values from 0 to 47
- tile_counts: int32 [8, 16], P('row', 'col'), may hold values from 24 to 96, as said below
- in_weight: bfloat16 [128, 256], replicated, may hold values from -0.5 to 0.5
- out_weight: bfloat16 [256, 172], replicated, may hold values from -0.375 to 0.375
- labels: int32 [8, 12288], P('row', 'col'), may hold values from 0 to 171
- loss_mask: int32 [8, 12288], P('row', 'col'), may hold values 0 or 1
Outputs:
- total_loss: float32 [], replicated
- grad_in: float32 [128, 256], replicated
- grad_out: float32 [256, 172], replicated
- grad_features: float32 [16, 6144, 128], P('col', 'row')
The draws below stay inside these ranges and needn't reach their ends.
Inputs may be any that keep to these rules, and one draw needn't show every extreme that they name: `tile_counts`: slots below a device's count are live, the rest are ignored; some device has all 96 slots live.
All inputs are finite; a program needn't handle non-finite values. No bound on the sum of `loss_mask` on one device may be relied on, other than what follows from the above.
Results may differ from the reference program's by a relative error of at most 0.0038.
The reference program's roundings to bfloat16 on the way (of `rounded_rows`, `hidden`, `log_grad`, `grad_pre` and `grad_feed`) count: a program that leaves them out, or rounds other values in their place, can miss the bound.
Values may be sent and summed in bfloat16 or wider, within the bound.
A program may use at most 128 MiB of HBM per device.

```python
import jax
import jax.numpy as jnp
from jax import lax

FIN = 128
HID = 256
CLS = 172
TILE = 128
CT = 48
TDEV = 96
RT = 96
RB = 12288
CB = 6144
NODES = 98304
N_ROW = 8
N_COL = 16


def draw_tile_counts(key, part):
    key = jax.random.fold_in(key, 5)
    first, second = jax.random.split(key)
    base = jax.random.randint(first, (N_ROW * N_COL,), TDEV // 4, TDEV // 2 + 1, dtype=jnp.int32)
    chosen = jax.random.randint(second, (), 0, N_ROW * N_COL, dtype=jnp.int32)
    filled = jnp.where(jnp.arange(N_ROW * N_COL, dtype=jnp.int32) == chosen, TDEV, base)
    return filled.reshape(N_ROW, N_COL).astype(jnp.int32)


def touch_ends(array, key, low, high):
    longest = array.shape.index(max(array.shape))
    spots = []
    for shift in (0, 1):
        where = [jax.random.randint(jax.random.fold_in(key, axis), (), 0, length) for axis, length in enumerate(array.shape)]
        where[longest] = (where[longest] + shift) % array.shape[longest]
        spots.append(tuple(where))
    return array.at[spots[0]].set(low).at[spots[1]].set(high)


def block_scale(key, extent, shards, least, largest):
    def one(axis_at, parts):
        steps = jax.random.uniform(jax.random.fold_in(jax.random.fold_in(key, 6), axis_at), (parts,), jnp.float32, least / len(shards), largest / len(shards))
        return jnp.repeat(jnp.exp(steps), extent[axis_at] // parts).reshape((-1,) + (1,) * (len(extent) - axis_at - 1))

    gain = one(*shards[0])
    for cut in shards[1:]:
        gain = gain * one(*cut)
    return gain


def bell_draw(key, dims, spread, reach, cuts=(), kind=jnp.bfloat16):
    entries = jax.random.normal(key, dims, jnp.float32) * spread
    if len(cuts) > 0:
        entries = block_scale(key, dims, cuts, -0.22, 0.18) * entries
    return jnp.clip(entries, min=-reach, max=reach).astype(kind)


def setup_inputs(seed: int = 0) -> dict:
    splits = jax.random.split(jax.random.key(seed), 10)
    return {
        "features": bell_draw(splits[0], (N_COL, CB, FIN), 1.0, 6.0, ((0, 16), (1, 8))),
        "tile_values": bell_draw(splits[1], (N_ROW, N_COL, TDEV, TILE, TILE), (TILE * N_COL * TDEV // (2 * RT)) ** -0.5, 0.1875, ((0, 8), (1, 16))),
        "tile_rows": touch_ends(jax.random.randint(splits[2], (N_ROW, N_COL, TDEV), 0, RT), jax.random.fold_in(splits[2], 1), 0, RT - 1).astype(jnp.int32),
        "tile_cols": touch_ends(jax.random.randint(splits[3], (N_ROW, N_COL, TDEV), 0, CT), jax.random.fold_in(splits[3], 1), 0, CT - 1).astype(jnp.int32),
        "tile_counts": draw_tile_counts(jax.random.fold_in(splits[9], 71), 0),
        "in_weight": bell_draw(splits[5], (FIN, HID), FIN ** -0.5, 0.5),
        "out_weight": bell_draw(splits[6], (HID, CLS), HID ** -0.5, 0.375),
        "labels": touch_ends(jax.random.randint(splits[7], (N_ROW, RB), 0, CLS), jax.random.fold_in(splits[7], 1), 0, CLS - 1).astype(jnp.int32),
        "loss_mask": touch_ends((jax.random.randint(splits[8], (N_ROW, RB), 0, 2) < 1).astype(jnp.int32), jax.random.fold_in(splits[8], 1), 0, 1),
    }


def live_mask(live_count, slot_count):
    return (jnp.arange(slot_count, dtype=jnp.int32) < live_count).astype(jnp.float32)[:, None, None]


def reference(features, tile_values, tile_rows, tile_cols, tile_counts, in_weight, out_weight, labels, loss_mask):
    xblocks = features.astype(jnp.float32).reshape(N_COL, CT, TILE, FIN)

    def forward_row(i):
        def advance(summed, j):
            values = tile_values[i, j].astype(jnp.float32)
            picked = xblocks[j][tile_cols[i, j]]
            product = jnp.einsum("tab,tbf->taf", values, picked) * live_mask(tile_counts[i, j], TDEV)
            return summed + jax.ops.segment_sum(product, tile_rows[i, j], num_segments=RT), None
        summed, _ = lax.scan(advance, jnp.zeros((RT, TILE, FIN), jnp.float32), jnp.arange(N_COL, dtype=jnp.int32))
        return summed.reshape(RB, FIN)

    aggregated = lax.map(forward_row, jnp.arange(N_ROW, dtype=jnp.int32)).reshape(NODES, FIN)
    rounded_rows = aggregated.astype(jnp.bfloat16)
    pre_act = jnp.dot(rounded_rows, in_weight, preferred_element_type=jnp.float32)
    sig_act = jax.nn.sigmoid(pre_act)
    hidden = (pre_act * sig_act).astype(jnp.bfloat16)
    logits = jnp.dot(hidden, out_weight, preferred_element_type=jnp.float32)
    log_norm = jnp.log(jnp.sum(jnp.exp(logits), axis=-1))
    flat_labels = labels.reshape(NODES)
    onehot = (flat_labels[:, None] == jnp.arange(CLS, dtype=jnp.int32)[None, :]).astype(jnp.float32)
    weights_row = loss_mask.reshape(NODES).astype(jnp.float32)
    counted = jnp.sum(weights_row)
    total_loss = jnp.sum(weights_row * (log_norm - jnp.sum(logits * onehot, axis=-1))) / counted
    log_grad = ((weights_row / counted)[:, None] * (jnp.exp(logits - log_norm[:, None]) - onehot)).astype(jnp.bfloat16)
    grad_out = jnp.dot(hidden.astype(jnp.float32).T, log_grad.astype(jnp.float32))
    grad_hidden = jnp.dot(log_grad, out_weight.T, preferred_element_type=jnp.float32)
    grad_pre = (grad_hidden * sig_act * (1.0 + pre_act * (1.0 - sig_act))).astype(jnp.bfloat16)
    grad_in = jnp.dot(rounded_rows.astype(jnp.float32).T, grad_pre.astype(jnp.float32))
    grad_feed = jnp.dot(grad_pre, in_weight.T, preferred_element_type=jnp.float32).astype(jnp.bfloat16)
    gblocks = grad_feed.astype(jnp.float32).reshape(N_ROW, RT, TILE, FIN)

    def backward_col(j):
        def advance(summed, i):
            values = tile_values[i, j].astype(jnp.float32)
            picked = gblocks[i][tile_rows[i, j]]
            product = jnp.einsum("tab,taf->tbf", values, picked) * live_mask(tile_counts[i, j], TDEV)
            return summed + jax.ops.segment_sum(product, tile_cols[i, j], num_segments=CT), None
        summed, _ = lax.scan(advance, jnp.zeros((CT, TILE, FIN), jnp.float32), jnp.arange(N_ROW, dtype=jnp.int32))
        return summed.reshape(CB, FIN)

    grad_features = lax.map(backward_col, jnp.arange(N_COL, dtype=jnp.int32))
    return total_loss, grad_in, grad_out, grad_features
```

```python
import functools

import jax
import jax.numpy as jnp
from jax import lax
from jax.experimental import pallas as pl
from jax.experimental.pallas import tpu as pltpu
from jax.sharding import PartitionSpec as P

F32, BF16, I32 = jnp.float32, jnp.bfloat16, jnp.int32
TILE = 128
SLOTS = 96
ROW_TILES = 96
COL_TILES = 48
OWN = 6
HALF = 3
CLS = 172
HID = 256
UNROLL = 8
N_SEMS = 112
WIRE2 = (BF16, BF16, BF16, BF16, BF16, BF16, F32)
WIRE4 = (BF16, BF16, BF16, BF16, BF16, BF16, F32)


def gather_blocks(copy, buf, block, ring, pair, first_src, work, landed):
    def part(dr, dp, half):
        return buf.at[pl.ds(block(dr, dp) * OWN + half * HALF, HALF)]

    def send(dr, dp, half, to):
        src = part(dr, dp, half)
        if (dr, dp) == (0, 0):
            src = first_src(half)
        c = copy(src, part(dr, dp, half), to)
        c.start()
        return c

    up, down, across = ring(1), ring(-1), pair
    own_up = {0: send(0, 0, 0, up)}
    own_down = {1: send(0, 0, 1, down)}
    own_pair = {0: send(0, 0, 0, across)}
    own_pair[1] = send(0, 0, 1, across)
    own_up[1] = send(0, 0, 1, up)
    own_down[0] = send(0, 0, 0, down)
    work(0)
    sends = [*own_up.values(), *own_down.values(), *own_pair.values()]
    own_up[0].wait_recv()
    far0 = send(-1, 0, 0, up)
    landed(-1, 0, 0)
    own_down[1].wait_recv()
    far1 = send(1, 0, 1, down)
    landed(1, 0, 1)
    work(1)
    beside = {}
    for half in (0, 1):
        own_pair[half].wait_recv()
        beside[0, half] = send(0, 1, half, up)
        beside[1, half] = send(0, 1, half, down)
        landed(0, 1, half)
    work(2)
    own_up[1].wait_recv()
    landed(-1, 0, 1)
    own_down[0].wait_recv()
    landed(1, 0, 0)
    far0.wait_recv()
    last0 = send(2, 0, 0, across)
    landed(2, 0, 0)
    far1.wait_recv()
    last1 = send(2, 0, 1, across)
    landed(2, 0, 1)
    work(3)
    for half in (0, 1):
        beside[0, half].wait_recv()
        landed(-1, 1, half)
        beside[1, half].wait_recv()
        landed(1, 1, half)
    last0.wait_recv()
    landed(2, 1, 0)
    last1.wait_recv()
    landed(2, 1, 1)
    return sends + [far0, far1, *beside.values(), last0, last1]


def scatter_blocks(copy, out, inn, ring, pair, source, work):
    up, down, across = ring(1), ring(-1), pair

    def halves(half):
        return pl.ds(half * HALF, HALF)

    def fill(slot, half, chip, *received):
        local = source(*chip)

        @pl.loop(half * HALF, half * HALF + HALF)
        def _(t):
            value = local(t)
            for n in received:
                value = value + inn[n][t].astype(F32)
            out[slot][t] = value.astype(out[slot].dtype)

    def send(slot, half, to, recv_slot):
        c = copy(out[slot].at[halves(half)], inn[recv_slot].at[halves(half)], to)
        c.start()
        return c

    z_far = []
    for half in (0, 1):
        fill(0, half, (2, 1))
        z_far.append(send(0, half, across, 0))
    x_up, x_down = [], []
    for half in (0, 1):
        fill(1, half, (1, 1))
        x_up.append(send(1, half, up, 1))
        fill(2, half, (-1, 1))
        x_down.append(send(2, half, down, 2))
    fill(3, 1, (1, 0))
    up_hi = send(3, 1, up, 3)
    fill(4, 0, (-1, 0))
    down_lo = send(4, 0, down, 4)
    work(0)
    z_far[0].wait_recv()
    fill(5, 0, (2, 0), 0)
    far_up = send(5, 0, up, 5)
    z_far[1].wait_recv()
    fill(5, 1, (2, 0), 0)
    far_down = send(5, 1, down, 5)
    work(1)
    z_near = []
    for half in (0, 1):
        x_up[half].wait_recv()
        x_down[half].wait_recv()
        fill(6, half, (0, 1), 1, 2)
        z_near.append(send(6, half, across, 6))
    far_up.wait_recv()
    fill(3, 0, (1, 0), 5)
    up_lo = send(3, 0, up, 3)
    far_down.wait_recv()
    fill(4, 1, (-1, 0), 5)
    down_hi = send(4, 1, down, 4)
    work(2)
    up_hi.wait_recv()
    down_lo.wait_recv()
    z_near[0].wait_recv()
    z_near[1].wait_recv()
    up_lo.wait_recv()
    down_hi.wait_recv()

    local = source(0, 0)

    def total(t):
        return local(t) + inn[3][t].astype(F32) + inn[4][t].astype(F32) + inn[6][t].astype(F32)

    return total, [*z_far, *x_up, *x_down, up_hi, down_lo, far_up, far_down, *z_near, up_lo, down_hi]


def order_slots(key, other, live, slots, tiles, idx, base):
    sub = lax.broadcasted_iota(I32, (slots, slots), 0)
    lane = lax.broadcasted_iota(I32, (slots, slots), 1)
    diag = sub == lane

    def column(v):
        return jnp.sum(jnp.where(diag, jnp.broadcast_to(v, (slots, slots)), 0), axis=1, keepdims=True)

    lane1 = lax.broadcasted_iota(I32, (1, slots), 1)
    sort_l = jnp.where(live > 0, key * TILE + lane1, tiles * TILE + lane1)
    sort_c, key_c, other_c, live_c = column(sort_l), column(key), column(other), column(live)
    rank_c = jnp.sum((jnp.broadcast_to(sort_l, (slots, slots)) < sort_c).astype(I32), axis=1, keepdims=True)

    def place(v):
        return jnp.sum(jnp.where(rank_c == lane, v, 0), axis=0, keepdims=True)

    idx[base : base + 1, 0:slots] = place(sub)
    idx[base + 1 : base + 2, 0:slots] = place(other_c)
    idx[base + 2 : base + 3, 0:slots] = place(key_c)
    below = jnp.sum(jnp.where(key_c <= lane, live_c, 0), axis=0, keepdims=True)
    same = jnp.sum(jnp.where(key_c == lane, live_c, 0), axis=0, keepdims=True)
    idx[base + 3 : base + 4, 0:slots] = jnp.maximum(below - 1, 0)
    idx[base + 4 : base + 5, 0:slots] = same


def tile_products(left, right, sums, where, base):
    def step(i, acc):
        for u in range(UNROLL):
            k = i * UNROLL + u
            prod = jnp.dot(left[where[base, k]], right[where[base + 1, k]], preferred_element_type=F32)
            before = jnp.maximum(k - 1, 0)
            keep = (where[base + 2, k] == where[base + 2, before]).astype(F32)
            acc = jnp.where(keep > 0, acc, 0.0) + prod
            sums[k] = acc
        return acc

    lax.fori_loop(0, SLOTS // UNROLL, step, jnp.zeros((TILE, TILE), F32))


def kernel(
    feat, vals_hbm, trow, tcol, tcnt, win, wout, lab, msk,
    loss_o, gin_o, gout_o, gf_o,
    vals, vals_t, feats, sums, core_out, core_in, *rest):
    out2, in2, out4, in4, rest = rest[0:7], rest[7:14], rest[14:21], rest[21:28], rest[28:]
    (grads,
    idx, where, lab_c, msk_c, wpad, rows_s, hid_s, lgrad_s, pre_s, gin_s, gout_s,
    m_part, y_in, m_y, x_in, z_all, c_out, c_in, final,
    cnt_out, cnt_in, send_sem, recv_sem, local_sem) = rest
    row, col = lax.axis_index("row"), lax.axis_index("col")
    zl, y = row // 4, row % 4
    zh, x, k = col // 8, (col // 2) % 4, col % 2

    def chip(zl_=zl, y_=y, zh_=zh, x_=x, k_=k):
        return {"row": zl_ * 4 + y_, "col": (zh_ * 4 + x_) * 2 + k_}

    def y_at(d):
        return chip(y_=(y + d + 4) % 4)

    def x_at(d):
        return chip(x_=(x + d + 4) % 4)

    z_others = [chip(zl_=1 - zl), chip(zh_=1 - zh), chip(zl_=1 - zl, zh_=1 - zh)]
    y_others = [y_at(d) for d in (1, 2, 3)]
    x_others = [x_at(d) for d in (1, 2, 3)]
    y_pair, x_pair, core = chip(zl_=1 - zl), chip(zh_=1 - zh), chip(k_=1 - k)

    used = []

    def copy(src, dst, to):
        n = len(used)
        used.append(n)
        return pltpu.make_async_remote_copy(
            src_ref=src, dst_ref=dst, send_sem=send_sem.at[n], recv_sem=recv_sem.at[n],
            device_id=to, device_id_type=pl.DeviceIdType.MESH,
        )

    def sent(src, dst, to):
        c = copy(src, dst, to)
        c.start()
        return c

    open_sends = []

    load_vals = pltpu.make_async_copy(vals_hbm.at[0, 0], vals, local_sem.at[0])
    load_vals.start()
    load_own = pltpu.make_async_copy(feat, feats.at[pl.ds(row * OWN, OWN)], local_sem.at[1])
    load_own.start()

    partners = [*y_others, *x_others, *z_others, core]
    barrier = pltpu.get_barrier_semaphore()
    for p in partners:
        pl.semaphore_signal(barrier, inc=1, device_id=p, device_id_type=pl.DeviceIdType.MESH)
    pl.semaphore_wait(barrier, len(partners))

    count_groups = [y_others, x_others, z_others, [core]]
    count_copies = []

    def count_send(stage):
        count_copies.append(
            [sent(cnt_out.at[stage], cnt_in.at[stage, n], to) for n, to in enumerate(count_groups[stage])]
        )

    def count_take(stage):
        for c in count_copies[stage]:
            c.wait_recv()
        value = cnt_out[stage]
        for n in range(len(count_groups[stage])):
            value = value + cnt_in[stage, n]
        cnt_out[stage + 1] = value

    def transpose(first, last):
        @pl.loop(first, last)
        def _(s):
            vals_t[s] = vals[s].astype(F32).T.astype(BF16)

    def prepare():
        slot = lax.broadcasted_iota(I32, (1, SLOTS), 1)
        live = (slot < tcnt[...]).astype(I32)
        idx[...] = jnp.zeros(idx.shape, I32)
        order_slots(trow[0], tcol[0], live, SLOTS, ROW_TILES, idx, 0)
        order_slots(tcol[0], trow[0], live, SLOTS, ROW_TILES, idx, 5)
        to_smem = pltpu.make_async_copy(idx, where, local_sem.at[2])
        to_smem.start()
        to_smem.wait()
        sub = lax.broadcasted_iota(I32, (TILE, TILE), 0)
        lane = lax.broadcasted_iota(I32, (TILE, TILE), 1)
        for t in range(OWN):
            for ref, dst in ((lab, lab_c), (msk, msk_c)):
                line = jnp.broadcast_to(ref[:, t * TILE : (t + 1) * TILE], (TILE, TILE))
                dst[t] = jnp.broadcast_to(
                    jnp.sum(jnp.where(sub == lane, line, 0), axis=1, keepdims=True), (TILE, TILE)
                )
        wpad[...] = jnp.zeros(wpad.shape, BF16)
        wpad[0:CLS] = wout[...]

    def work1(stage):
        if stage == 0:
            cnt_out[0] = jnp.broadcast_to(jnp.sum(msk[...].astype(F32), axis=1, keepdims=True), (8, TILE))
            count_send(0)
            prepare()
            load_vals.wait()
        elif stage == 1:
            transpose(0, 8)
        elif stage == 2:
            count_take(0)
            count_send(1)
            transpose(8, 16)
        else:
            transpose(16, 24)
            count_take(1)
            count_send(2)

    open_sends += gather_blocks(
        copy, feats, lambda dr, dp: (zl + dp) % 2 * 4 + (y + dr + 4) % 4, y_at, y_pair,
        lambda half: feat.at[pl.ds(half * HALF, HALF)], work1, lambda dr, dp, half: None,
    )
    load_own.wait()

    tile_products(vals, feats, sums, where, 0)

    def row_sum(tile):
        return sums[where[3, tile]] * (where[4, tile] > 0).astype(F32)

    def col_sum(tile):
        return sums[where[8, tile]] * (where[9, tile] > 0).astype(F32)

    def chip_index(dr, dp):
        return (zh + dp) % 2 * 4 + (x + dr + 4) % 4

    classes = [(2, 1), (1, 1), (-1, 1), (1, 0), (-1, 0), (2, 0), (0, 1), (0, 0)]
    core_copies = {}
    for n, (dr, dp) in enumerate(classes):
        base = (chip_index(dr, dp) * 2 + 1 - k) * OWN

        @pl.loop(0, OWN)
        def _(t, n=n, base=base):
            core_out[n, t] = row_sum(base + t)

        core_copies[dr, dp] = sent(core_out.at[n], core_in.at[n], core)
    taken = set()

    def source2(dr, dp):
        if (dr, dp) not in taken:
            taken.add((dr, dp))
            core_copies[dr, dp].wait_recv()
        base = (chip_index(dr, dp) * 2 + k) * OWN
        return lambda t: row_sum(base + t) + core_in[classes.index((dr, dp)), t]

    def work2(stage):
        if stage == 0:
            transpose(24, 40)
        elif stage == 1:
            count_take(2)
            count_send(3)
            transpose(40, 56)
        else:
            transpose(56, 76)
            count_take(3)

    total2, sends2 = scatter_blocks(copy, out2, in2, x_at, x_pair, source2, work2)
    open_sends += [*sends2, *core_copies.values()]

    counted = cnt_out[4][0:1, 0:1]
    lane = lax.broadcasted_iota(I32, (TILE, HID), 1)

    def head(t, loss):
        rounded = total2(t).astype(BF16)
        rows_s[t] = rounded
        pre = jnp.dot(rounded, win[...], preferred_element_type=F32)
        sig = jax.nn.sigmoid(pre)
        hidden = (pre * sig).astype(BF16)
        hid_s[t] = hidden
        logits = lax.dot_general(hidden, wpad[...], (((1,), (1,)), ((), ())), preferred_element_type=F32)
        log_norm = jnp.log(jnp.sum(jnp.where(lane < CLS, jnp.exp(logits), 0.0), axis=1, keepdims=True))
        onehot = (lane == lab_c[t][:, 0:1]).astype(F32)
        weight = msk_c[t][:, 0:1].astype(F32)
        loss = loss + weight * (log_norm - jnp.sum(logits * onehot, axis=1, keepdims=True))
        prob = jnp.where(lane < CLS, jnp.exp(logits - log_norm), 0.0)
        log_grad = ((weight / counted) * (prob - onehot)).astype(BF16)
        lgrad_s[t] = log_grad
        back = jnp.dot(log_grad, wpad[...], preferred_element_type=F32)
        grad_pre = (back * sig * (1.0 + pre * (1.0 - sig))).astype(BF16)
        pre_s[t] = grad_pre
        feed = lax.dot_general(grad_pre, win[...], (((1,), (1,)), ((), ())), preferred_element_type=F32)
        grads[col * OWN + t] = feed.astype(BF16)
        return loss

    loss = lax.fori_loop(0, OWN, head, jnp.zeros((TILE, 1), F32))
    loss = jnp.sum(loss, axis=0, keepdims=True) / counted

    steps = {}

    def weight_grads():
        over = (((0,), (0,)), ((), ()))
        gin_s[...] = jnp.zeros((TILE, HID), F32)
        gout_s[...] = jnp.zeros((HID, HID), F32)

        @pl.loop(0, OWN)
        def _(t):
            gin_s[...] += lax.dot_general(rows_s[t], pre_s[t], over, preferred_element_type=F32)
            gout_s[...] += lax.dot_general(lgrad_s[t], hid_s[t], over, preferred_element_type=F32)

        sub = lax.broadcasted_iota(I32, (8, HID), 0)
        lane = lax.broadcasted_iota(I32, (8, HID), 1)
        gout_s[HID - 8 : HID] = jnp.where((sub == 7) & (lane == 0), jnp.broadcast_to(loss, (8, HID)), gout_s[HID - 8 : HID])
        for n in range(16):
            for r in range(0, 24, 8):
                at = n * 24 + r
                m_part[n // 4, n % 4, r : r + 8] = gin_s[at : at + 8] if at < TILE else gout_s[at - TILE : at - TILE + 8]
        steps["y"] = [
            sent(m_part.at[(y + d) % 4], y_in.at[d - 1], to) for d, to in zip((1, 2, 3), y_others)
        ]

    def sum_y():
        for c in steps["y"]:
            c.wait_recv()
        for n in range(4):
            m_y[n] = m_part[y, n] + y_in[0, n] + y_in[1, n] + y_in[2, n]
        steps["x"] = [sent(m_y.at[(x + d) % 4], x_in.at[d - 1], to) for d, to in zip((1, 2, 3), x_others)]

    def sum_x():
        for c in steps["x"]:
            c.wait_recv()
        me = zh * 2 + zl
        z_all[me] = m_y[x] + x_in[0] + x_in[1] + x_in[2]
        steps["z"] = [sent(z_all.at[me], z_all.at[me], to) for to in z_others]

    def sum_z():
        for c in steps["z"]:
            c.wait_recv()
        c_out[...] = (z_all[0] + z_all[1]) + (z_all[2] + z_all[3])
        steps["core"] = [sent(c_out, c_in, core)]

    def sum_core():
        for c in steps["core"]:
            c.wait_recv()
        final[x, y] = c_out[...] + c_in[...]
        steps["spread_y"] = [sent(final.at[x, y], final.at[x, y], to) for to in y_others]

    def spread_x():
        for c in steps["spread_y"]:
            c.wait_recv()
        steps["spread_x"] = [sent(final.at[x], final.at[x], to) for to in x_others]

    hand_over = []

    def hand(dr, dp, half):
        at = pl.ds((chip_index(dr, dp) * 2 + k) * OWN + half * HALF, HALF)
        hand_over.append(sent(grads.at[at], grads.at[at], core))

    def work3(stage):
        if stage == 0:
            for half in (0, 1):
                hand(0, 0, half)
            weight_grads()
            transpose(76, 86)
        elif stage == 1:
            transpose(86, 96)
        elif stage == 3:
            sum_y()

    open_sends += gather_blocks(
        copy, grads, lambda dr, dp: chip_index(dr, dp) * 2 + k, x_at, x_pair,
        lambda half: grads.at[pl.ds(col * OWN + half * HALF, HALF)], work3, hand,
    )
    for c in hand_over:
        c.wait_recv()
    open_sends += hand_over

    tile_products(vals_t, grads, sums, where, 5)

    def source4(dr, dp):
        base = ((zl + dp) % 2 * 4 + (y + dr + 4) % 4) * OWN
        return lambda t: col_sum(base + t)

    def work4(stage):
        if stage == 0:
            sum_x()
        elif stage == 1:
            sum_z()
            sum_core()
        else:
            spread_x()

    total4, sends4 = scatter_blocks(copy, out4, in4, y_at, y_pair, source4, work4)
    open_sends += sends4

    @pl.loop(0, OWN)
    def _(t):
        gf_o[t] = total4(t)

    for c in steps["spread_x"]:
        c.wait_recv()
    for n in range(16):
        for r in range(0, 24, 8):
            at = n * 24 + r
            piece = final[n % 4, n // 4, r : r + 8]
            if at < TILE:
                gin_o[at : at + 8] = piece
            else:
                put = min(8, CLS - (at - TILE))
                if put > 0:
                    gout_o[at - TILE : at - TILE + put] = piece[0:put]
                if at == TILE + HID - 8:
                    loss_o[...] = jnp.broadcast_to(piece[7:8, 0:1], loss_o.shape)

    for group in steps.values():
        open_sends += group
    for group in count_copies:
        open_sends += group
    for c in open_sends:
        c.wait_send()


def hand_out(loss, gin, gout, gf, loss_o, gin_o, gout_o, gf_o):
    loss_o[0] = loss[0, 0]
    gin_o[...] = gin[...]
    gout_o[...] = gout[...]
    gf_o[...] = gf[...]


def shards(
    features,
    tile_values,
    tile_rows,
    tile_cols,
    tile_counts,
    in_weight,
    out_weight,
    labels,
    loss_mask,
):
    vmem = pl.BlockSpec(memory_space=pltpu.VMEM)
    smem = pl.BlockSpec(memory_space=pltpu.SMEM)
    hbm = pl.BlockSpec(memory_space=pl.ANY)
    block = (OWN, TILE, TILE)
    loss, grad_in, grad_out, grad_features = pl.pallas_call(
        kernel,
        out_shape=(
            jax.ShapeDtypeStruct((8, TILE), F32),
            jax.ShapeDtypeStruct((TILE, HID), F32),
            jax.ShapeDtypeStruct((CLS, HID), F32),
            jax.ShapeDtypeStruct(block, F32),
        ),
        in_specs=[hbm, hbm, vmem, vmem, vmem, vmem, vmem, vmem, vmem],
        out_specs=(vmem, vmem, vmem, vmem),
        scratch_shapes=[
            pltpu.VMEM((SLOTS, TILE, TILE), BF16),
            pltpu.VMEM((SLOTS, TILE, TILE), BF16),
            pltpu.VMEM((COL_TILES, TILE, TILE), BF16),
            pltpu.VMEM((SLOTS, TILE, TILE), F32),
            pltpu.VMEM((8, *block), F32),
            pltpu.VMEM((8, *block), F32),
            *(pltpu.VMEM(block, wire) for kinds in (WIRE2, WIRE2, WIRE4, WIRE4) for wire in kinds),
            pltpu.VMEM((ROW_TILES, TILE, TILE), BF16),
            pltpu.VMEM((16, TILE), I32),
            pltpu.SMEM((16, TILE), I32),
            pltpu.VMEM(block, I32),
            pltpu.VMEM(block, I32),
            pltpu.VMEM((HID, HID), BF16),
            pltpu.VMEM((OWN, TILE, TILE), BF16),
            pltpu.VMEM((OWN, TILE, HID), BF16),
            pltpu.VMEM((OWN, TILE, HID), BF16),
            pltpu.VMEM((OWN, TILE, HID), BF16),
            pltpu.VMEM((TILE, HID), F32),
            pltpu.VMEM((HID, HID), F32),
            pltpu.VMEM((4, 4, 24, HID), F32),
            pltpu.VMEM((3, 4, 24, HID), F32),
            pltpu.VMEM((4, 24, HID), F32),
            pltpu.VMEM((3, 24, HID), F32),
            pltpu.VMEM((4, 24, HID), F32),
            pltpu.VMEM((24, HID), F32),
            pltpu.VMEM((24, HID), F32),
            pltpu.VMEM((4, 4, 24, HID), F32),
            pltpu.VMEM((5, 8, TILE), F32),
            pltpu.VMEM((4, 3, 8, TILE), F32),
            pltpu.SemaphoreType.DMA((N_SEMS,)),
            pltpu.SemaphoreType.DMA((N_SEMS,)),
            pltpu.SemaphoreType.DMA((3,)),
        ],
        compiler_params=pltpu.CompilerParams(
            collective_id=0, has_side_effects=True, vmem_limit_bytes=56 * 1024 * 1024
        ),
        name="graph_layer",
    )(
        features.reshape(OWN, TILE, TILE),
        tile_values,
        tile_rows[0],
        tile_cols[0],
        tile_counts,
        in_weight,
        out_weight.T,
        labels,
        loss_mask,
    )
    shapes = (loss, grad_in, grad_out, grad_features)
    loss, grad_in, grad_out, grad_features = pl.pallas_call(
        hand_out,
        out_shape=(jax.ShapeDtypeStruct((1,), F32), *(jax.ShapeDtypeStruct(s.shape, F32) for s in shapes[1:])),
        in_specs=[vmem] * 4,
        out_specs=(smem, vmem, vmem, vmem),
        name="hand_out",
    )(*shapes)
    return loss.reshape(()), grad_in, grad_out.T, grad_features.reshape(1, OWN * TILE, TILE)


def solution(mesh):
    placed = (
        P("col", "row", None),
        P("row", "col", None, None, None),
        P("row", "col", None),
        P("row", "col", None),
        P("row", "col"),
        P(),
        P(),
        P("row", "col"),
        P("row", "col"),
    )
    return jax.shard_map(
        shards,
        mesh=mesh,
        in_specs=placed,
        out_specs=(P(), P(), P(), P("col", "row", None)),
        check_vma=False,
    )
```

```python
import jax
import jax.numpy as jnp
from jax import lax
from jax.experimental import pallas as pl
from jax.experimental.pallas import tpu as pltpu
from jax.sharding import PartitionSpec as P

F32, BF16, I32 = jnp.float32, jnp.bfloat16, jnp.int32
TILE = 128
WIDE = 64
SLOTS = 96
ROW_TILES = 96
COL_TILES = 48
OWN = 6
HALF = 3
CLS = 172
CLS_ROWS = 176
HID = 256
UNROLL = 48
N_SEMS = 184
MESSAGES = ("far_pair", "side_up", "side_down", "free_up", "free_down", "far", "near_pair", "late_up", "late_down")
WIRE2 = (BF16, BF16, BF16, BF16, BF16, BF16, F32, F32, F32)
WIRE4 = (BF16, BF16, BF16, BF16, BF16, BF16, BF16, BF16, BF16)
NT = (((1,), (1,)), ((), ()))


def gather(copy, buf, block, ring, pair, landed):
    def send(dr, dp, half, to):
        at = buf.at[pl.ds(block(dr, dp) * OWN + half * HALF, HALF)]
        return copy(at, at, to)

    up, down, across = ring(1), ring(-1), pair
    up0, down1, pair0 = send(0, 0, 0, up), send(0, 0, 1, down), send(0, 0, 0, across)
    up1, down0, pair1 = send(0, 0, 1, up), send(0, 0, 0, down), send(0, 0, 1, across)
    yield "own"
    for c in (up0, down1, pair0, up1, down0, pair1):
        c.wait_send()
    yield "left"
    up0.wait_recv()
    far0 = send(-1, 0, 0, up)
    landed(-1, 0, 0)
    down1.wait_recv()
    far1 = send(1, 0, 1, down)
    landed(1, 0, 1)
    yield "far"
    beside = []
    for half, c in enumerate((pair0, pair1)):
        c.wait_recv()
        beside.append((send(0, 1, half, up), send(0, 1, half, down)))
        landed(0, 1, half)
    yield "beside"
    up1.wait_recv()
    landed(-1, 0, 1)
    down0.wait_recv()
    landed(1, 0, 0)
    far0.wait_recv()
    last0 = send(2, 0, 0, across)
    landed(2, 0, 0)
    far1.wait_recv()
    last1 = send(2, 0, 1, across)
    landed(2, 0, 1)
    yield "last"
    for half in (0, 1):
        beside[half][0].wait_recv()
        landed(-1, 1, half)
        beside[half][1].wait_recv()
        landed(1, 1, half)
    last0.wait_recv()
    landed(2, 1, 0)
    last1.wait_recv()
    landed(2, 1, 1)
    yield "done"


def scatter(copy, out, inn, chunk, ring, pair, source, result):
    up, down, across = ring(1), ring(-1), pair
    both = (0, OWN)
    halves = ((0, HALF), (HALF, OWN))

    def fill(name, span, chip, *received):
        local = source(*chip)
        ref = out[name]

        for t in range(*span):
            value = local(t)
            for n in received:
                value = value + inn[n][chunk, t].astype(F32)
            ref[chunk, t] = value.astype(ref.dtype)

    def send(name, span, to):
        at = pl.ds(span[0], span[1] - span[0])
        return copy(out[name].at[chunk, at], inn[name].at[chunk, at], to)

    far_pair = []
    for span in halves:
        fill("far_pair", span, (2, 1))
        far_pair.append(send("far_pair", span, across))
    fill("side_up", both, (1, 1))
    side_up = send("side_up", both, up)
    fill("side_down", both, (-1, 1))
    side_down = send("side_down", both, down)
    fill("free_up", halves[1], (1, 0))
    free_up = send("free_up", halves[1], up)
    fill("free_down", halves[0], (-1, 0))
    free_down = send("free_down", halves[0], down)
    yield "start"
    far_pair[0].wait_recv()
    fill("far", halves[0], (2, 0), "far_pair")
    far_up = send("far", halves[0], up)
    far_pair[1].wait_recv()
    fill("far", halves[1], (2, 0), "far_pair")
    far_down = send("far", halves[1], down)
    yield "far"
    side_up.wait_recv()
    side_down.wait_recv()
    near = []
    for span in halves:
        fill("near_pair", span, (0, 1), "side_up", "side_down")
        near.append(send("near_pair", span, across))
    yield "near"
    far_up.wait_recv()
    fill("late_up", halves[0], (1, 0), "far")
    late_up = send("late_up", halves[0], up)
    far_down.wait_recv()
    fill("late_down", halves[1], (-1, 0), "far")
    late_down = send("late_down", halves[1], down)
    yield "late"
    for c in (free_up, free_down, near[0], near[1], late_up, late_down):
        c.wait_recv()
    local = source(0, 0)
    for t in range(OWN):
        from_below = inn["late_up" if t < HALF else "free_up"][chunk, t]
        from_above = inn["free_down" if t < HALF else "late_down"][chunk, t]
        value = local(t) + from_below.astype(F32) + from_above.astype(F32)
        result(t, value + inn["near_pair"][chunk, t].astype(F32))
    yield "done"


def order_slots(key, other, live, slots, tiles, idx, base):
    sub = lax.broadcasted_iota(I32, (slots, slots), 0)
    lane = lax.broadcasted_iota(I32, (slots, slots), 1)
    diag = sub == lane

    def column(v):
        return jnp.sum(jnp.where(diag, jnp.broadcast_to(v, (slots, slots)), 0), axis=1, keepdims=True)

    lane1 = lax.broadcasted_iota(I32, (1, slots), 1)
    sort_l = jnp.where(live > 0, key * TILE + lane1, tiles * TILE + lane1)
    sort_c, key_c, other_c, live_c = column(sort_l), column(key), column(other), column(live)
    rank_c = jnp.sum((jnp.broadcast_to(sort_l, (slots, slots)) < sort_c).astype(I32), axis=1, keepdims=True)

    def place(v):
        return jnp.sum(jnp.where(rank_c == lane, v, 0), axis=0, keepdims=True)

    idx[base : base + 1, 0:slots] = place(sub)
    idx[base + 1 : base + 2, 0:slots] = place(other_c)
    idx[base + 2 : base + 3, 0:slots] = place(key_c)
    below = jnp.sum(jnp.where(key_c <= lane, live_c, 0), axis=0, keepdims=True)
    same = jnp.sum(jnp.where(key_c == lane, live_c, 0), axis=0, keepdims=True)
    idx[base + 3 : base + 4, 0:slots] = jnp.maximum(below - 1, 0)
    idx[base + 4 : base + 5, 0:slots] = same


def tile_products(product, sums, where, base):
    def step(i, acc):
        for u in range(UNROLL):
            k = i * UNROLL + u
            prod = product(where[base, k], where[base + 1, k])
            keep = where[base + 2, k] == where[base + 2, jnp.maximum(k - 1, 0)]
            acc = jnp.where(keep, acc, 0.0) + prod
            sums[k] = acc
        return acc

    lax.fori_loop(0, SLOTS // UNROLL, step, jnp.zeros((WIDE, TILE), F32))


class Copy:
    def __init__(self, src, dst, to, send_sem, recv_sem):
        self.copy = pltpu.make_async_remote_copy(
            src_ref=src, dst_ref=dst, send_sem=send_sem, recv_sem=recv_sem,
            device_id=to, device_id_type=pl.DeviceIdType.MESH,
        )
        self.sending = True
        self.copy.start()

    def wait_recv(self):
        self.copy.wait_recv()

    def wait_send(self):
        if self.sending:
            self.sending = False
            self.copy.wait_send()


def run_to(phase, step):
    while next(phase) != step:
        pass


def kernel(
    feat, vals_hbm, trow_h, tcol_h, tcnt_h, win_h, wout_h, lab_h, msk_h,
    loss_o, gin_o, gout_o, gf_o,
    trow, tcol, tcnt, win, wout, lab, msk,
    feat_v, vals, vals_t, xt_a, xt_b, gt_a, gt_b, sums, core_out, core_in, gf_t,
    idx, where, win_t, wpad, wpad_t, rows_s, hid_s, lgrad_s, pre_s, gin_s, gout_s,
    m_part, y_in, m_y, x_in, z_all, c_out, c_in, final,
    cnt_out, cnt_in, send_sem, recv_sem, local_sem, *messages,
):
    row, col = lax.axis_index("row"), lax.axis_index("col")
    zl, y = row // 4, row % 4
    zh, x, k = col // 8, (col // 2) % 4, col % 2
    xt, gt = (xt_a, xt_b), (gt_a, gt_b)
    out2, in2, out4, in4 = (dict(zip(MESSAGES, messages[n : n + 9])) for n in (0, 9, 18, 27))

    def chip(zl_=zl, y_=y, zh_=zh, x_=x, k_=k):
        return {"row": zl_ * 4 + y_, "col": (zh_ * 4 + x_) * 2 + k_}

    def y_at(d):
        return chip(y_=(y + d + 4) % 4)

    def x_at(d):
        return chip(x_=(x + d + 4) % 4)

    def row_chip(dr, dp):
        return (zl + dp) % 2 * 4 + (y + dr + 4) % 4

    def col_chip(dr, dp):
        return (zh + dp) % 2 * 4 + (x + dr + 4) % 4

    z_others = [chip(zl_=1 - zl), chip(zh_=1 - zh), chip(zl_=1 - zl, zh_=1 - zh)]
    y_others = [y_at(d) for d in (1, 2, 3)]
    x_others = [x_at(d) for d in (1, 2, 3)]
    y_pair, x_pair, core = chip(zl_=1 - zl), chip(zh_=1 - zh), chip(k_=1 - k)

    copies = []

    def copy(src, dst, to):
        n = len(copies)
        copies.append(Copy(src, dst, to, send_sem.at[n], recv_sem.at[n]))
        return copies[n]

    load_own = pltpu.make_async_copy(feat, feat_v, local_sem.at[0])
    load_own.start()
    load_vals = pltpu.make_async_copy(vals_hbm.at[0, 0], vals, local_sem.at[1])
    load_vals.start()
    pairs = ((trow_h, trow), (tcol_h, tcol), (tcnt_h, tcnt), (win_h, win), (wout_h, wout), (lab_h, lab), (msk_h, msk))
    loads = [pltpu.make_async_copy(src, dst, local_sem.at[3 + n]) for n, (src, dst) in enumerate(pairs)]
    for c in loads:
        c.start()

    partners = [*y_others, *x_others, *z_others, core]
    barrier = pltpu.get_barrier_semaphore()
    for p in partners:
        pl.semaphore_signal(barrier, inc=1, device_id=p, device_id_type=pl.DeviceIdType.MESH)
    load_own.wait()
    for t in range(OWN):
        turned = feat_v[t].astype(F32).T.astype(BF16)
        xt_a[row * OWN + t] = turned[0:WIDE]
        xt_b[row * OWN + t] = turned[WIDE:]
    pl.semaphore_wait(barrier, len(partners))

    count_groups = [y_others, x_others, z_others, [core]]
    count_copies = []

    def count_send(stage):
        count_copies.append(
            [copy(cnt_out.at[stage], cnt_in.at[stage, n], to) for n, to in enumerate(count_groups[stage])]
        )

    def count_take(stage):
        for c in count_copies[stage]:
            c.wait_recv()
        value = cnt_out[stage]
        for n in range(len(count_groups[stage])):
            value = value + cnt_in[stage, n]
        cnt_out[stage + 1] = value

    def prepare_slots():
        slot = lax.broadcasted_iota(I32, (1, SLOTS), 1)
        live = (slot < tcnt[...]).astype(I32)
        idx[...] = jnp.zeros(idx.shape, I32)
        order_slots(trow[...], tcol[...], live, SLOTS, ROW_TILES, idx, 0)
        order_slots(tcol[...], trow[...], live, SLOTS, ROW_TILES, idx, 5)
        to_smem = pltpu.make_async_copy(idx, where, local_sem.at[2])
        to_smem.start()
        to_smem.wait()

    def prepare_weights():
        win_t[...] = win[...].astype(F32).T.astype(BF16)
        wpad[...] = jnp.zeros(wpad.shape, BF16)
        wpad[0:CLS] = wout[...]
        wpad_t[...] = wpad[...].astype(F32).T.astype(BF16)
        lgrad_s[...] = jnp.zeros(lgrad_s.shape, BF16)

    def row_sum(chunk, tile):
        return sums[chunk, where[3, tile]] * (where[4, tile] > 0).astype(F32)

    def col_sum(chunk, tile):
        return sums[chunk, where[8, tile]] * (where[9, tile] > 0).astype(F32)

    def forward(chunk):
        def product(slot, other):
            return jnp.dot(xt[chunk][other], vals_t[slot], preferred_element_type=F32)

        tile_products(product, sums.at[chunk], where, 0)

    def backward(chunk):
        def product(slot, other):
            return jnp.dot(gt[chunk][other], vals[slot], preferred_element_type=F32)

        tile_products(product, sums.at[chunk], where, 5)

    classes = [(2, 1), (1, 1), (-1, 1), (1, 0), (-1, 0), (2, 0), (0, 1), (0, 0)]
    core_copies = {}

    def core_send(chunk):
        for n, (dr, dp) in enumerate(classes):
            base = (col_chip(dr, dp) * 2 + 1 - k) * OWN
            for t in range(OWN):
                core_out[chunk, n, t] = row_sum(chunk, base + t)
            core_copies[chunk, dr, dp] = copy(core_out.at[chunk, n], core_in.at[chunk, n], core)

    def forward_source(chunk):
        taken = set()

        def source(dr, dp):
            if (dr, dp) not in taken:
                taken.add((dr, dp))
                core_copies[chunk, dr, dp].wait_recv()
            base, n = (col_chip(dr, dp) * 2 + k) * OWN, classes.index((dr, dp))
            return lambda t: row_sum(chunk, base + t) + core_in[chunk, n, t]

        return source

    def take_rows(chunk):
        def result(t, value):
            lanes = slice(t % 2 * TILE, t % 2 * TILE + TILE)
            rows_s[t // 2, chunk * WIDE : chunk * WIDE + WIDE, lanes] = value.astype(BF16)

        return result

    gather_a, gather_b = (
        gather(copy, xt[c], row_chip, y_at, y_pair, lambda dr, dp, half: None) for c in (0, 1)
    )
    scatter_a, scatter_b = (
        scatter(copy, out2, in2, c, x_at, x_pair, forward_source(c), take_rows(c)) for c in (0, 1)
    )
    run_to(gather_a, "own")
    for c in loads:
        c.wait()
    cnt_out[0] = jnp.broadcast_to(jnp.sum(msk[...].astype(F32), axis=1, keepdims=True), (8, TILE))
    count_send(0)
    run_to(gather_a, "left")
    run_to(gather_b, "own")
    prepare_slots()
    run_to(gather_a, "beside")
    run_to(gather_b, "far")
    count_take(0)
    count_send(1)
    run_to(gather_a, "last")
    run_to(gather_b, "beside")
    prepare_weights()
    load_vals.wait()

    @pl.loop(0, SLOTS, unroll=8)
    def _(n):
        vals_t[n] = vals[n].T

    run_to(gather_b, "last")
    run_to(gather_a, "done")
    forward(0)
    core_send(0)
    count_take(1)
    count_send(2)
    run_to(gather_b, "done")
    forward(1)
    core_send(1)
    run_to(scatter_a, "start")
    run_to(scatter_b, "start")
    run_to(scatter_a, "far")
    run_to(scatter_a, "near")
    count_take(2)
    count_send(3)
    run_to(scatter_b, "far")
    run_to(scatter_a, "late")
    run_to(scatter_b, "near")
    run_to(scatter_b, "late")
    count_take(3)
    run_to(scatter_a, "done")
    run_to(scatter_b, "done")

    counted = cnt_out[4][0:1, 0:1]
    sub = lax.broadcasted_iota(I32, (CLS_ROWS, 2 * TILE), 0)
    loss = jnp.zeros((1, 2 * TILE), F32)
    for j in range(OWN // 2):
        nodes = slice(j * 2 * TILE, (j + 1) * 2 * TILE)
        pre = jnp.dot(win_t[...], rows_s[j], preferred_element_type=F32)
        sig = jax.nn.sigmoid(pre)
        hidden = (pre * sig).astype(BF16)
        hid_s[j] = hidden
        logits = jnp.dot(wpad[0:CLS_ROWS], hidden, preferred_element_type=F32)
        log_norm = jnp.log(jnp.sum(jnp.where(sub < CLS, jnp.exp(logits), 0.0), axis=0, keepdims=True))
        onehot = (sub == lab[:, nodes]).astype(F32)
        weight = msk[:, nodes].astype(F32)
        loss = loss + weight * (log_norm - jnp.sum(logits * onehot, axis=0, keepdims=True))
        prob = jnp.where(sub < CLS, jnp.exp(logits - log_norm), 0.0)
        lgrad_s[j, 0:CLS_ROWS] = ((weight / counted) * (prob - onehot)).astype(BF16)
        back = jnp.dot(wpad_t[...], lgrad_s[j], preferred_element_type=F32)
        grad_pre = (back * sig * (1.0 + pre * (1.0 - sig))).astype(BF16)
        pre_s[j] = grad_pre
        feed = jnp.dot(win[...], grad_pre, preferred_element_type=F32).astype(BF16)
        for c in (0, 1):
            for u in (0, 1):
                gt[c][col * OWN + 2 * j + u] = feed[c * WIDE : (c + 1) * WIDE, u * TILE : (u + 1) * TILE]
    loss = jnp.sum(loss, axis=1, keepdims=True) / counted

    steps = {}

    def weight_grads():
        gin_s[...] = jnp.zeros((TILE, HID), F32)
        gout_s[...] = jnp.zeros((HID, HID), F32)

        @pl.loop(0, OWN // 2)
        def _(j):
            gin_s[...] += lax.dot_general(rows_s[j], pre_s[j], NT, preferred_element_type=F32)
            gout_s[...] += lax.dot_general(lgrad_s[j], hid_s[j], NT, preferred_element_type=F32)

        sub = lax.broadcasted_iota(I32, (8, HID), 0)
        lane = lax.broadcasted_iota(I32, (8, HID), 1)
        tail = gout_s[HID - 8 : HID]
        gout_s[HID - 8 : HID] = jnp.where((sub == 7) & (lane == 0), jnp.broadcast_to(loss, (8, HID)), tail)
        for n in range(16):
            for r in range(0, 24, 8):
                at = n * 24 + r
                piece = gin_s[at : at + 8] if at < TILE else gout_s[at - TILE : at - TILE + 8]
                m_part[n // 4, n % 4, r : r + 8] = piece
        steps["y"] = [copy(m_part.at[(y + d) % 4], y_in.at[d - 1], to) for d, to in zip((1, 2, 3), y_others)]

    def sum_y():
        for c in steps["y"]:
            c.wait_recv()
        for n in range(4):
            m_y[n] = m_part[y, n] + y_in[0, n] + y_in[1, n] + y_in[2, n]
        steps["x"] = [copy(m_y.at[(x + d) % 4], x_in.at[d - 1], to) for d, to in zip((1, 2, 3), x_others)]

    def sum_x():
        for c in steps["x"]:
            c.wait_recv()
        me = zh * 2 + zl
        z_all[me] = m_y[x] + x_in[0] + x_in[1] + x_in[2]
        steps["z"] = [copy(z_all.at[me], z_all.at[me], to) for to in z_others]

    def sum_z():
        for c in steps["z"]:
            c.wait_recv()
        c_out[...] = (z_all[0] + z_all[1]) + (z_all[2] + z_all[3])
        steps["core"] = [copy(c_out, c_in, core)]

    def sum_core():
        for c in steps["core"]:
            c.wait_recv()
        final[x, y] = c_out[...] + c_in[...]
        steps["spread_y"] = [copy(final.at[x, y], final.at[x, y], to) for to in y_others]

    def spread_x():
        for c in steps["spread_y"]:
            c.wait_recv()
        steps["spread_x"] = [copy(final.at[x], final.at[x], to) for to in x_others]

    handed = ([], [])

    def hand(chunk):
        def landed(dr, dp, half):
            at = gt[chunk].at[pl.ds((col_chip(dr, dp) * 2 + k) * OWN + half * HALF, HALF)]
            handed[chunk].append(copy(at, at, core))

        return landed

    def take_hand(chunk):
        for c in handed[chunk]:
            c.wait_recv()

    def take_grads(chunk):
        def result(t, value):
            gf_t[t, chunk * WIDE : chunk * WIDE + WIDE] = value

        return result

    def backward_source(chunk):
        def source(dr, dp):
            base = row_chip(dr, dp) * OWN
            return lambda t: col_sum(chunk, base + t)

        return source

    gather_a, gather_b = (
        gather(copy, gt[c], lambda dr, dp: col_chip(dr, dp) * 2 + k, x_at, x_pair, hand(c)) for c in (0, 1)
    )
    scatter_a, scatter_b = (
        scatter(copy, out4, in4, c, y_at, y_pair, backward_source(c), take_grads(c)) for c in (0, 1)
    )
    run_to(gather_a, "own")
    for half in (0, 1):
        hand(0)(0, 0, half)
    run_to(gather_a, "left")
    run_to(gather_b, "own")
    for half in (0, 1):
        hand(1)(0, 0, half)
    weight_grads()
    run_to(gather_a, "beside")
    run_to(gather_b, "far")
    run_to(gather_a, "last")
    run_to(gather_b, "beside")
    run_to(gather_b, "last")
    sum_y()
    run_to(gather_a, "done")
    take_hand(0)
    backward(0)
    run_to(scatter_a, "start")
    sum_x()
    run_to(gather_b, "done")
    take_hand(1)
    backward(1)
    run_to(scatter_b, "start")
    run_to(scatter_a, "far")
    run_to(scatter_a, "near")
    sum_z()
    run_to(scatter_b, "far")
    sum_core()
    run_to(scatter_a, "late")
    run_to(scatter_b, "near")
    spread_x()
    run_to(scatter_b, "late")
    run_to(scatter_a, "done")
    run_to(scatter_b, "done")
    for t in range(OWN):
        gf_o[t] = gf_t[t].T

    for c in steps["spread_x"]:
        c.wait_recv()
    for n in range(16):
        for r in range(0, 24, 8):
            at = n * 24 + r
            piece = final[n % 4, n // 4, r : r + 8]
            if at < TILE:
                gin_o[at : at + 8] = piece
            else:
                put = min(8, CLS - (at - TILE))
                if put > 0:
                    gout_o[at - TILE : at - TILE + put] = piece[0:put]
                if at == TILE + HID - 8:
                    loss_o[...] = jnp.broadcast_to(piece[7:8, 0:1], loss_o.shape)

    for c in copies:
        c.wait_send()


def hand_out(loss, gin, gout, gf, loss_o, gin_o, gout_o, gf_o):
    loss_o[0] = loss[0, 0]
    gin_o[...] = gin[...]
    gout_o[...] = gout[...]
    gf_o[...] = gf[...]


def shards(
    features,
    tile_values,
    tile_rows,
    tile_cols,
    tile_counts,
    in_weight,
    out_weight,
    labels,
    loss_mask,
):
    vmem = pl.BlockSpec(memory_space=pltpu.VMEM)
    smem = pl.BlockSpec(memory_space=pltpu.SMEM)
    hbm = pl.BlockSpec(memory_space=pl.ANY)
    block = (OWN, TILE, TILE)
    loss, grad_in, grad_out, grad_features = pl.pallas_call(
        kernel,
        out_shape=(
            pltpu.VMEM((8, TILE), F32),
            pltpu.VMEM((TILE, HID), F32),
            pltpu.VMEM((CLS, HID), F32),
            pltpu.VMEM(block, F32),
        ),
        in_specs=[hbm] * 9,
        out_specs=(vmem, vmem, vmem, vmem),
        scratch_shapes=[
            pltpu.VMEM((1, SLOTS), I32),
            pltpu.VMEM((1, SLOTS), I32),
            pltpu.VMEM((1, 1), I32),
            pltpu.VMEM((TILE, HID), BF16),
            pltpu.VMEM((CLS, HID), BF16),
            pltpu.VMEM((1, OWN * TILE), I32),
            pltpu.VMEM((1, OWN * TILE), I32),
            pltpu.VMEM(block, BF16),
            pltpu.VMEM((SLOTS, TILE, TILE), BF16),
            pltpu.VMEM((SLOTS, TILE, TILE), BF16),
            *(pltpu.VMEM((COL_TILES, WIDE, TILE), BF16) for _ in range(2)),
            *(pltpu.VMEM((ROW_TILES, WIDE, TILE), BF16) for _ in range(2)),
            pltpu.VMEM((2, SLOTS, WIDE, TILE), F32),
            pltpu.VMEM((2, 8, OWN, WIDE, TILE), F32),
            pltpu.VMEM((2, 8, OWN, WIDE, TILE), F32),
            pltpu.VMEM(block, F32),
            pltpu.VMEM((16, TILE), I32),
            pltpu.SMEM((16, TILE), I32),
            pltpu.VMEM((HID, TILE), BF16),
            pltpu.VMEM((HID, HID), BF16),
            pltpu.VMEM((HID, HID), BF16),
            pltpu.VMEM((OWN // 2, TILE, 2 * TILE), BF16),
            pltpu.VMEM((OWN // 2, HID, 2 * TILE), BF16),
            pltpu.VMEM((OWN // 2, HID, 2 * TILE), BF16),
            pltpu.VMEM((OWN // 2, HID, 2 * TILE), BF16),
            pltpu.VMEM((TILE, HID), F32),
            pltpu.VMEM((HID, HID), F32),
            pltpu.VMEM((4, 4, 24, HID), F32),
            pltpu.VMEM((3, 4, 24, HID), F32),
            pltpu.VMEM((4, 24, HID), F32),
            pltpu.VMEM((3, 24, HID), F32),
            pltpu.VMEM((4, 24, HID), F32),
            pltpu.VMEM((24, HID), F32),
            pltpu.VMEM((24, HID), F32),
            pltpu.VMEM((4, 4, 24, HID), F32),
            pltpu.VMEM((5, 8, TILE), F32),
            pltpu.VMEM((4, 3, 8, TILE), F32),
            pltpu.SemaphoreType.DMA((N_SEMS,)),
            pltpu.SemaphoreType.DMA((N_SEMS,)),
            pltpu.SemaphoreType.DMA((10,)),
            *(pltpu.VMEM((2, OWN, WIDE, TILE), wire) for kinds in (WIRE2, WIRE2, WIRE4, WIRE4) for wire in kinds),
        ],
        compiler_params=pltpu.CompilerParams(
            collective_id=0, has_side_effects=True, vmem_limit_bytes=56 * 1024 * 1024
        ),
        name="graph_layer",
    )(
        features.reshape(OWN, TILE, TILE),
        tile_values,
        tile_rows[0],
        tile_cols[0],
        tile_counts,
        in_weight,
        out_weight.T,
        labels,
        loss_mask,
    )
    shapes = [pltpu.with_memory_space_constraint(v, pltpu.VMEM) for v in (loss, grad_in, grad_out, grad_features)]
    loss, grad_in, grad_out, grad_features = pl.pallas_call(
        hand_out,
        out_shape=(jax.ShapeDtypeStruct((1,), F32), *(jax.ShapeDtypeStruct(s.shape, F32) for s in shapes[1:])),
        in_specs=[vmem] * 4,
        out_specs=(smem, vmem, vmem, vmem),
        name="hand_out",
    )(*shapes)
    return loss.reshape(()), grad_in, grad_out.T, grad_features.reshape(1, OWN * TILE, TILE)


def solution(mesh):
    placed = (
        P("col", "row", None),
        P("row", "col", None, None, None),
        P("row", "col", None),
        P("row", "col", None),
        P("row", "col"),
        P(),
        P(),
        P("row", "col"),
        P("row", "col"),
    )
    return jax.shard_map(
        shards,
        mesh=mesh,
        in_specs=placed,
        out_specs=(P(), P(), P(), P("col", "row", None)),
        check_vma=False,
    )
```

```python
import jax
import jax.numpy as jnp
from jax import lax
from jax.experimental import pallas as pl
from jax.experimental.pallas import tpu as pltpu
from jax.sharding import PartitionSpec as P

F32, BF16, I32 = jnp.float32, jnp.bfloat16, jnp.int32
TILE = 128
CHUNKS = ((0, 64), (64, 64))
SLOTS = 96
ROW_TILES = 96
COL_TILES = 48
OWN = 6
HALF = 3
CLS = 172
CLS_ROWS = 176
HID = 256
UNROLL = 48
N_SEMS = 86
WIDER2 = (True, True)
WIDER4 = (True, True)
FAR_PAIR, SIDE_UP, SIDE_DOWN, FREE, FAR, LATE, NEAR = range(7)
FORWARD = (
    ("gather", 0, "own"), ("gather", 1, "own"), ("gather", 0, "far"), ("slots", 0, ""),
    ("weights", 0, ""), ("gather", 1, "far"), ("gather", 0, "beside"), ("turn", 0, ""),
    ("gather", 0, "last"), ("count", 0, ""), ("gather", 1, "beside"), ("gather", 1, "last"),
    ("gather", 0, "done"), ("products", 0, ""), ("count", 1, ""), ("cores", 0, ""),
    ("gather", 1, "done"), ("products", 1, ""), ("scatter", 0, "start"), ("cores", 1, ""),
    ("scatter", 1, "start"), ("count", 2, ""), ("scatter", 0, "far"), ("scatter", 0, "near"),
    ("count", 3, ""), ("scatter", 1, "far"), ("scatter", 1, "near"), ("scatter", 0, "late"),
    ("scatter", 1, "late"), ("scatter", 0, "done"), ("scatter", 1, "done"),
)
BACKWARD = (
    ("gather", 0, "own"), ("small", 0, ""), ("gather", 1, "own"), ("gather", 0, "far"),
    ("gather", 1, "far"), ("gather", 0, "beside"), ("gather", 0, "last"), ("small", 1, ""),
    ("gather", 1, "beside"), ("gather", 1, "last"), ("small", 2, ""), ("gather", 0, "done"),
    ("handed", 0, ""), ("products", 0, ""), ("scatter", 0, "start"), ("gather", 1, "done"),
    ("small", 3, ""), ("handed", 1, ""), ("products", 1, ""), ("small", 4, ""),
    ("scatter", 0, "far"), ("scatter", 1, "start"), ("scatter", 0, "near"), ("scatter", 1, "far"),
    ("small", 5, ""), ("scatter", 1, "near"), ("scatter", 0, "late"), ("scatter", 1, "late"),
    ("scatter", 0, "done"), ("scatter", 1, "done"),
)
NT = (((1,), (1,)), ((), ()))


def gather(copy, counter, buf, block, ring, pair, landed):
    def expect(blocks):
        return counter(buf.at[0 : blocks * OWN])

    def send(dr, dp, half, to, recv):
        at = buf.at[pl.ds(block(dr, dp) * OWN + half * HALF, HALF)]
        copy(at, at, to, sent, recv)

    up, down, across = ring(1), ring(-1), pair
    sent, first, beside, far, rest = expect(7), expect(1), expect(1), expect(1), expect(4)
    send(0, 0, 0, up, first)
    send(0, 0, 1, down, first)
    send(0, 0, 0, across, beside)
    send(0, 0, 1, up, rest)
    send(0, 0, 0, down, rest)
    send(0, 0, 1, across, beside)
    yield "own"
    first.wait()
    send(-1, 0, 0, up, far)
    send(1, 0, 1, down, far)
    landed(-1, 0, 0)
    landed(1, 0, 1)
    yield "far"
    beside.wait()
    for half in (0, 1):
        send(0, 1, half, up, rest)
        send(0, 1, half, down, rest)
    landed(0, 1)
    yield "beside"
    far.wait()
    send(2, 0, 0, across, rest)
    send(2, 0, 1, across, rest)
    landed(2, 0)
    yield "last"
    rest.wait()
    landed(-1, 0, 1)
    landed(1, 0, 0)
    landed(-1, 1)
    landed(1, 1)
    landed(2, 1)
    yield "done"


def scatter(copy, counter, out, inn, out_near, in_near, ring, pair, source, result):
    up, down, across = ring(1), ring(-1), pair
    both = (0, OWN)
    low, high = (0, HALF), (HALF, OWN)

    def fill(ref, span, chip, *received):
        local = source(*chip)
        for t in range(*span):
            value = local(t)
            for n in received:
                value = value + inn[n, t].astype(F32)
            ref[t] = value.astype(ref.dtype)

    def send(slot, span, to, recv):
        at = pl.ds(span[0], span[1] - span[0])
        copy(out.at[slot, at], inn.at[slot, at], to, sent, recv)

    sent, sent_near = counter(out.at[0:NEAR]), counter(out_near)
    far_pair = [counter(inn.at[FAR_PAIR, a:b]) for a, b in (low, high)]
    side, free, far, late = counter(inn.at[0:2]), counter(inn.at[0]), counter(inn.at[0]), counter(inn.at[0])
    near = counter(in_near)
    for n, span in enumerate((low, high)):
        fill(out.at[FAR_PAIR], span, (2, 1))
        send(FAR_PAIR, span, across, far_pair[n])
    fill(out.at[SIDE_UP], both, (1, 1))
    send(SIDE_UP, both, up, side)
    fill(out.at[SIDE_DOWN], both, (-1, 1))
    send(SIDE_DOWN, both, down, side)
    fill(out.at[FREE], high, (1, 0))
    send(FREE, high, up, free)
    fill(out.at[FREE], low, (-1, 0))
    send(FREE, low, down, free)
    yield "start"
    far_pair[0].wait()
    fill(out.at[FAR], low, (2, 0), FAR_PAIR)
    send(FAR, low, up, far)
    far_pair[1].wait()
    fill(out.at[FAR], high, (2, 0), FAR_PAIR)
    send(FAR, high, down, far)
    yield "far"
    side.wait()
    for a, b in (low, high):
        fill(out_near, (a, b), (0, 1), SIDE_UP, SIDE_DOWN)
        copy(out_near.at[a:b], in_near.at[a:b], across, sent_near, near)
    yield "near"
    far.wait()
    fill(out.at[LATE], low, (1, 0), FAR)
    send(LATE, low, up, late)
    fill(out.at[LATE], high, (-1, 0), FAR)
    send(LATE, high, down, late)
    yield "late"
    free.wait()
    near.wait()
    late.wait()
    local = source(0, 0)
    for t in range(OWN):
        value = local(t) + inn[FREE, t].astype(F32) + inn[LATE, t].astype(F32)
        result(t, value + in_near[t].astype(F32))
    yield "done"


def order_slots(key, other, live, slots, tiles, idx, base):
    sub = lax.broadcasted_iota(I32, (slots, slots), 0)
    lane = lax.broadcasted_iota(I32, (slots, slots), 1)
    diag = sub == lane

    def column(v):
        return jnp.sum(jnp.where(diag, jnp.broadcast_to(v, (slots, slots)), 0), axis=1, keepdims=True)

    lane1 = lax.broadcasted_iota(I32, (1, slots), 1)
    sort_l = jnp.where(live > 0, key * TILE + lane1, tiles * TILE + lane1)
    sort_c, key_c, other_c, live_c = column(sort_l), column(key), column(other), column(live)
    rank_c = jnp.sum((jnp.broadcast_to(sort_l, (slots, slots)) < sort_c).astype(I32), axis=1, keepdims=True)

    def place(v):
        return jnp.sum(jnp.where(rank_c == lane, v, 0), axis=0, keepdims=True)

    idx[base : base + 1, 0:slots] = place(sub)
    idx[base + 1 : base + 2, 0:slots] = place(other_c)
    idx[base + 2 : base + 3, 0:slots] = place(key_c)
    below = jnp.sum(jnp.where(key_c <= lane, live_c, 0), axis=0, keepdims=True)
    same = jnp.sum(jnp.where(key_c == lane, live_c, 0), axis=0, keepdims=True)
    idx[base + 3 : base + 4, 0:slots] = jnp.maximum(below - 1, 0)
    idx[base + 4 : base + 5, 0:slots] = same


def tile_products(product, sums, where, base):
    def step(i, acc):
        for u in range(UNROLL):
            k = i * UNROLL + u
            prod = product(where[base, k], where[base + 1, k])
            keep = where[base + 2, k] == where[base + 2, jnp.maximum(k - 1, 0)]
            acc = jnp.where(keep, acc, 0.0) + prod
            sums[k] = acc
        return acc

    lax.fori_loop(0, SLOTS // UNROLL, step, jnp.zeros(sums.shape[1:], F32))


class Counter:
    def __init__(self, sem, like):
        self.sem, self.like = sem, like
        self.waiting = True

    def wait(self):
        if self.waiting:
            self.waiting = False
            pltpu.make_async_copy(self.like, self.like, self.sem).wait()


def run_to(phase, step):
    while next(phase) != step:
        pass


def kernel(
    feat, vals_hbm, trow_h, tcol_h, tcnt_h, win_h, wout_h, lab_h, msk_h,
    loss_o, gin_o, gout_o, gf_o,
    trow, tcol, tcnt, win, wout, lab, msk,
    feat_v, vals, vals_t, gf_t,
    idx, where, win_t, wpad, wpad_t, rows_s, hid_s, lgrad_s, pre_s, gin_s, gout_s,
    m_part, y_in, m_y, x_in, z_all, c_out, c_in, final,
    cnt_out, cnt_in, sems, local_sem, *parts,
):
    row, col = lax.axis_index("row"), lax.axis_index("col")
    zl, y = row // 4, row % 4
    zh, x, k = col // 8, (col // 2) % 4, col % 2
    count = len(CHUNKS)
    xt, gt, sums, core_out, core_in = (parts[n * count : (n + 1) * count] for n in range(5))
    out2, in2, out4, in4, near_out2, near_in2, near_out4, near_in4 = (
        parts[n * count : (n + 1) * count] for n in range(5, 13)
    )

    def chip(zl_=zl, y_=y, zh_=zh, x_=x, k_=k):
        return {"row": zl_ * 4 + y_, "col": (zh_ * 4 + x_) * 2 + k_}

    def y_at(d):
        return chip(y_=(y + d + 4) % 4)

    def x_at(d):
        return chip(x_=(x + d + 4) % 4)

    def row_chip(dr, dp):
        return (zl + dp) % 2 * 4 + (y + dr + 4) % 4

    def col_chip(dr, dp):
        return (zh + dp) % 2 * 4 + (x + dr + 4) % 4

    z_others = [chip(zl_=1 - zl), chip(zh_=1 - zh), chip(zl_=1 - zl, zh_=1 - zh)]
    y_others = [y_at(d) for d in (1, 2, 3)]
    x_others = [x_at(d) for d in (1, 2, 3)]
    y_pair, x_pair, core = chip(zl_=1 - zl), chip(zh_=1 - zh), chip(k_=1 - k)

    counters = []

    def counter(like):
        counters.append(Counter(sems.at[len(counters)], like))
        return counters[-1]

    def copy(src, dst, to, send, recv):
        pltpu.make_async_remote_copy(
            src_ref=src, dst_ref=dst, send_sem=send.sem, recv_sem=recv.sem,
            device_id=to, device_id_type=pl.DeviceIdType.MESH,
        ).start()

    load_own = pltpu.make_async_copy(feat, feat_v, local_sem.at[0])
    load_own.start()
    load_vals = pltpu.make_async_copy(vals_hbm.at[0, 0], vals, local_sem.at[1])
    load_vals.start()
    pairs = ((trow_h, trow), (tcol_h, tcol), (tcnt_h, tcnt), (win_h, win), (wout_h, wout), (lab_h, lab), (msk_h, msk))
    loads = [pltpu.make_async_copy(src, dst, local_sem.at[3 + n]) for n, (src, dst) in enumerate(pairs)]
    for c in loads:
        c.start()

    partners = [*y_others, *x_others, *z_others, core]
    barrier = pltpu.get_barrier_semaphore()
    for p in partners:
        pl.semaphore_signal(barrier, inc=1, device_id=p, device_id_type=pl.DeviceIdType.MESH)
    load_own.wait()
    for t in range(OWN):
        turned = feat_v[t].astype(F32).T.astype(BF16)
        for c, (first, width) in enumerate(CHUNKS):
            xt[c][row * OWN + t] = turned[first : first + width]
    pl.semaphore_wait(barrier, len(partners))

    count_groups = [y_others, x_others, z_others, [core]]
    count_copies = []

    def count_send(stage):
        group = count_groups[stage]
        like = cnt_in.at[stage, 0 : len(group)]
        send, recv = counter(like), counter(like)
        for n, to in enumerate(group):
            copy(cnt_out.at[stage], cnt_in.at[stage, n], to, send, recv)
        count_copies.append(recv)

    def count_take(stage):
        count_copies[stage].wait()
        value = cnt_out[stage]
        for n in range(len(count_groups[stage])):
            value = value + cnt_in[stage, n]
        cnt_out[stage + 1] = value

    def prepare_slots():
        slot = lax.broadcasted_iota(I32, (1, SLOTS), 1)
        live = (slot < tcnt[...]).astype(I32)
        idx[...] = jnp.zeros(idx.shape, I32)
        order_slots(trow[...], tcol[...], live, SLOTS, ROW_TILES, idx, 0)
        order_slots(tcol[...], trow[...], live, SLOTS, ROW_TILES, idx, 5)
        to_smem = pltpu.make_async_copy(idx, where, local_sem.at[2])
        to_smem.start()
        to_smem.wait()

    def prepare_weights():
        win_t[...] = win[...].astype(F32).T.astype(BF16)
        wpad[...] = jnp.zeros(wpad.shape, BF16)
        wpad[0:CLS] = wout[...]
        wpad_t[...] = wpad[...].astype(F32).T.astype(BF16)
        lgrad_s[...] = jnp.zeros(lgrad_s.shape, BF16)

    def row_sum(chunk, tile):
        return sums[chunk][where[3, tile]] * (where[4, tile] > 0).astype(F32)

    def col_sum(chunk, tile):
        return sums[chunk][where[8, tile]] * (where[9, tile] > 0).astype(F32)

    def forward(chunk):
        def product(slot, other):
            return jnp.dot(xt[chunk][other], vals_t[slot], preferred_element_type=F32)

        tile_products(product, sums[chunk], where, 0)

    def backward(chunk):
        def product(slot, other):
            return jnp.dot(gt[chunk][other], vals[slot], preferred_element_type=F32)

        tile_products(product, sums[chunk], where, 5)

    classes = [(2, 1), (1, 1), (-1, 1), (1, 0), (-1, 0), (2, 0), (0, 1), (0, 0)]
    core_first, core_rest = {}, {}

    def core_send(chunk):
        send = counter(core_out[chunk])
        core_first[chunk], core_rest[chunk] = counter(core_in[chunk].at[0]), counter(core_in[chunk].at[1:8])
        for n, (dr, dp) in enumerate(classes):
            base = (col_chip(dr, dp) * 2 + 1 - k) * OWN
            for t in range(OWN):
                core_out[chunk][n, t] = row_sum(chunk, base + t)
            recv = core_rest[chunk] if n else core_first[chunk]
            copy(core_out[chunk].at[n], core_in[chunk].at[n], core, send, recv)

    def forward_source(chunk):
        def source(dr, dp):
            base, n = (col_chip(dr, dp) * 2 + k) * OWN, classes.index((dr, dp))
            (core_rest if n else core_first)[chunk].wait()
            return lambda t: row_sum(chunk, base + t) + core_in[chunk][n, t]

        return source

    def take_rows(chunk):
        first, width = CHUNKS[chunk]

        def result(t, value):
            lanes = slice(t % 2 * TILE, t % 2 * TILE + TILE)
            rows_s[t // 2, first : first + width, lanes] = value.astype(BF16)

        return result

    def turn_tiles():
        load_vals.wait()

        @pl.loop(0, SLOTS, unroll=8)
        def _(n):
            vals_t[n] = vals[n].T

    def count_step(stage):
        if stage == 0:
            cnt_out[0] = jnp.broadcast_to(jnp.sum(msk[...].astype(F32), axis=1, keepdims=True), (8, TILE))
        else:
            count_take(stage - 1)
        count_send(stage)

    gathers = [gather(copy, counter, xt[c], row_chip, y_at, y_pair, lambda *chip: None) for c in range(count)]
    scatters = [
        scatter(copy, counter, out2[c], in2[c], near_out2[c], near_in2[c], x_at, x_pair, forward_source(c), take_rows(c)) for c in range(count)
    ]
    loaded = False
    for what, c, step in FORWARD:
        if what in ("count", "slots", "weights") and not loaded:
            loaded = True
            for load in loads:
                load.wait()
        if what == "gather":
            run_to(gathers[c], step)
        elif what == "scatter":
            run_to(scatters[c], step)
        elif what == "products":
            forward(c)
        elif what == "cores":
            core_send(c)
        elif what == "count":
            count_step(c)
        elif what == "slots":
            prepare_slots()
        elif what == "weights":
            prepare_weights()
        elif what == "turn":
            turn_tiles()
    count_take(3)

    counted = cnt_out[4][0:1, 0:1]
    sub = lax.broadcasted_iota(I32, (CLS_ROWS, 2 * TILE), 0)
    loss = jnp.zeros((1, 2 * TILE), F32)
    for j in range(OWN // 2):
        nodes = slice(j * 2 * TILE, (j + 1) * 2 * TILE)
        pre = jnp.dot(win_t[...], rows_s[j], preferred_element_type=F32)
        sig = jax.nn.sigmoid(pre)
        hidden = (pre * sig).astype(BF16)
        hid_s[j] = hidden
        logits = jnp.dot(wpad[0:CLS_ROWS], hidden, preferred_element_type=F32)
        log_norm = jnp.log(jnp.sum(jnp.where(sub < CLS, jnp.exp(logits), 0.0), axis=0, keepdims=True))
        onehot = (sub == lab[:, nodes]).astype(F32)
        weight = msk[:, nodes].astype(F32)
        loss = loss + weight * (log_norm - jnp.sum(logits * onehot, axis=0, keepdims=True))
        prob = jnp.where(sub < CLS, jnp.exp(logits - log_norm), 0.0)
        lgrad_s[j, 0:CLS_ROWS] = ((weight / counted) * (prob - onehot)).astype(BF16)
        back = jnp.dot(wpad_t[...], lgrad_s[j], preferred_element_type=F32)
        grad_pre = (back * sig * (1.0 + pre * (1.0 - sig))).astype(BF16)
        pre_s[j] = grad_pre
        feed = jnp.dot(win[...], grad_pre, preferred_element_type=F32).astype(BF16)
        for c, (first, width) in enumerate(CHUNKS):
            for u in (0, 1):
                gt[c][col * OWN + 2 * j + u] = feed[first : first + width, u * TILE : (u + 1) * TILE]
    loss = jnp.sum(loss, axis=1, keepdims=True) / counted

    steps = {}

    def spread(name, like, moves):
        send, steps[name] = counter(like), counter(like)
        for src, dst, to in moves:
            copy(src, dst, to, send, steps[name])

    def weight_grads():
        gin_s[...] = jnp.zeros((TILE, HID), F32)
        gout_s[...] = jnp.zeros((HID, HID), F32)

        @pl.loop(0, OWN // 2)
        def _(j):
            gin_s[...] += lax.dot_general(rows_s[j], pre_s[j], NT, preferred_element_type=F32)
            gout_s[...] += lax.dot_general(lgrad_s[j], hid_s[j], NT, preferred_element_type=F32)

        sub = lax.broadcasted_iota(I32, (8, HID), 0)
        lane = lax.broadcasted_iota(I32, (8, HID), 1)
        tail = gout_s[HID - 8 : HID]
        gout_s[HID - 8 : HID] = jnp.where((sub == 7) & (lane == 0), jnp.broadcast_to(loss, (8, HID)), tail)
        for n in range(16):
            for r in range(0, 24, 8):
                at = n * 24 + r
                piece = gin_s[at : at + 8] if at < TILE else gout_s[at - TILE : at - TILE + 8]
                m_part[n // 4, n % 4, r : r + 8] = piece
        spread("y", y_in, [(m_part.at[(y + d) % 4], y_in.at[d - 1], to) for d, to in zip((1, 2, 3), y_others)])

    def sum_y():
        steps["y"].wait()
        for n in range(4):
            m_y[n] = m_part[y, n] + y_in[0, n] + y_in[1, n] + y_in[2, n]
        spread("x", x_in, [(m_y.at[(x + d) % 4], x_in.at[d - 1], to) for d, to in zip((1, 2, 3), x_others)])

    def sum_x():
        steps["x"].wait()
        me = zh * 2 + zl
        z_all[me] = m_y[x] + x_in[0] + x_in[1] + x_in[2]
        spread("z", z_all.at[0:3], [(z_all.at[me], z_all.at[me], to) for to in z_others])

    def sum_z():
        steps["z"].wait()
        c_out[...] = (z_all[0] + z_all[1]) + (z_all[2] + z_all[3])
        spread("core", c_in, [(c_out, c_in, core)])

    def sum_core():
        steps["core"].wait()
        final[x, y] = c_out[...] + c_in[...]
        spread("spread_y", final.at[0, 0:3], [(final.at[x, y], final.at[x, y], to) for to in y_others])

    def spread_x():
        steps["spread_y"].wait()
        spread("spread_x", final.at[0:3], [(final.at[x], final.at[x], to) for to in x_others])

    handed = [(counter(gt[c].at[0 : 8 * OWN]), counter(gt[c].at[0 : 8 * OWN])) for c in range(count)]

    def hand(chunk):
        def landed(dr, dp, half=None):
            first, size = (0, OWN) if half is None else (half * HALF, HALF)
            at = gt[chunk].at[pl.ds((col_chip(dr, dp) * 2 + k) * OWN + first, size)]
            copy(at, at, core, *handed[chunk])

        return landed

    def take_grads(chunk):
        first, width = CHUNKS[chunk]

        def result(t, value):
            gf_t[t, first : first + width] = value

        return result

    def backward_source(chunk):
        def source(dr, dp):
            base = row_chip(dr, dp) * OWN
            return lambda t: col_sum(chunk, base + t)

        return source

    gathers = [
        gather(copy, counter, gt[c], lambda dr, dp: col_chip(dr, dp) * 2 + k, x_at, x_pair, hand(c)) for c in range(count)
    ]
    scatters = [
        scatter(copy, counter, out4[c], in4[c], near_out4[c], near_in4[c], y_at, y_pair, backward_source(c), take_grads(c)) for c in range(count)
    ]
    small = (weight_grads, sum_y, sum_x, sum_z, sum_core, spread_x)
    for what, c, step in BACKWARD:
        if what == "gather":
            run_to(gathers[c], step)
            if step == "own":
                hand(c)(0, 0)
        elif what == "scatter":
            run_to(scatters[c], step)
        elif what == "handed":
            handed[c][1].wait()
        elif what == "products":
            backward(c)
        elif what == "small":
            small[c]()
    for t in range(OWN):
        gf_o[t] = gf_t[t].T

    steps["spread_x"].wait()
    for n in range(16):
        for r in range(0, 24, 8):
            at = n * 24 + r
            piece = final[n % 4, n // 4, r : r + 8]
            if at < TILE:
                gin_o[at : at + 8] = piece
            else:
                put = min(8, CLS - (at - TILE))
                if put > 0:
                    gout_o[at - TILE : at - TILE + put] = piece[0:put]
                if at == TILE + HID - 8:
                    loss_o[...] = jnp.broadcast_to(piece[7:8, 0:1], loss_o.shape)

    for c in counters:
        c.wait()


def hand_out(loss, gin, gout, gf, loss_o, gin_o, gout_o, gf_o):
    loss_o[0] = loss[0, 0]
    gin_o[...] = gin[...]
    gout_o[...] = gout[...]
    gf_o[...] = gf[...]


def shards(
    features,
    tile_values,
    tile_rows,
    tile_cols,
    tile_counts,
    in_weight,
    out_weight,
    labels,
    loss_mask,
):
    vmem = pl.BlockSpec(memory_space=pltpu.VMEM)
    smem = pl.BlockSpec(memory_space=pltpu.SMEM)
    hbm = pl.BlockSpec(memory_space=pl.ANY)
    block = (OWN, TILE, TILE)
    loss, grad_in, grad_out, grad_features = pl.pallas_call(
        kernel,
        out_shape=(
            pltpu.VMEM((8, TILE), F32),
            pltpu.VMEM((TILE, HID), F32),
            pltpu.VMEM((CLS, HID), F32),
            pltpu.VMEM(block, F32),
        ),
        in_specs=[hbm] * 9,
        out_specs=(vmem, vmem, vmem, vmem),
        scratch_shapes=[
            pltpu.VMEM((1, SLOTS), I32),
            pltpu.VMEM((1, SLOTS), I32),
            pltpu.VMEM((1, 1), I32),
            pltpu.VMEM((TILE, HID), BF16),
            pltpu.VMEM((CLS, HID), BF16),
            pltpu.VMEM((1, OWN * TILE), I32),
            pltpu.VMEM((1, OWN * TILE), I32),
            pltpu.VMEM(block, BF16),
            pltpu.VMEM((SLOTS, TILE, TILE), BF16),
            pltpu.VMEM((SLOTS, TILE, TILE), BF16),
            pltpu.VMEM(block, F32),
            pltpu.VMEM((16, TILE), I32),
            pltpu.SMEM((16, TILE), I32),
            pltpu.VMEM((HID, TILE), BF16),
            pltpu.VMEM((HID, HID), BF16),
            pltpu.VMEM((HID, HID), BF16),
            pltpu.VMEM((OWN // 2, TILE, 2 * TILE), BF16),
            pltpu.VMEM((OWN // 2, HID, 2 * TILE), BF16),
            pltpu.VMEM((OWN // 2, HID, 2 * TILE), BF16),
            pltpu.VMEM((OWN // 2, HID, 2 * TILE), BF16),
            pltpu.VMEM((TILE, HID), F32),
            pltpu.VMEM((HID, HID), F32),
            pltpu.VMEM((4, 4, 24, HID), F32),
            pltpu.VMEM((3, 4, 24, HID), F32),
            pltpu.VMEM((4, 24, HID), F32),
            pltpu.VMEM((3, 24, HID), F32),
            pltpu.VMEM((4, 24, HID), F32),
            pltpu.VMEM((24, HID), F32),
            pltpu.VMEM((24, HID), F32),
            pltpu.VMEM((4, 4, 24, HID), F32),
            pltpu.VMEM((5, 8, TILE), F32),
            pltpu.VMEM((4, 3, 8, TILE), F32),
            pltpu.SemaphoreType.DMA((N_SEMS,)),
            pltpu.SemaphoreType.DMA((10,)),
            *(pltpu.VMEM((COL_TILES, width, TILE), BF16) for _, width in CHUNKS),
            *(pltpu.VMEM((ROW_TILES, width, TILE), BF16) for _, width in CHUNKS),
            *(pltpu.VMEM((SLOTS, width, TILE), F32) for _, width in CHUNKS),
            *(pltpu.VMEM((8, OWN, width, TILE), F32) for _, width in CHUNKS),
            *(pltpu.VMEM((8, OWN, width, TILE), F32) for _, width in CHUNKS),
            *(pltpu.VMEM((NEAR, OWN, width, TILE), BF16) for _ in range(4) for _, width in CHUNKS),
            *(
                pltpu.VMEM((OWN, width, TILE), F32 if wider[c] else BF16)
                for wider in (WIDER2, WIDER2, WIDER4, WIDER4)
                for c, (_, width) in enumerate(CHUNKS)
            ),
        ],
        compiler_params=pltpu.CompilerParams(
            collective_id=0, has_side_effects=True, vmem_limit_bytes=56 * 1024 * 1024
        ),
        name="graph_layer",
    )(
        features.reshape(OWN, TILE, TILE),
        tile_values,
        tile_rows[0],
        tile_cols[0],
        tile_counts,
        in_weight,
        out_weight.T,
        labels,
        loss_mask,
    )
    shapes = [pltpu.with_memory_space_constraint(v, pltpu.VMEM) for v in (loss, grad_in, grad_out, grad_features)]
    loss, grad_in, grad_out, grad_features = pl.pallas_call(
        hand_out,
        out_shape=(jax.ShapeDtypeStruct((1,), F32), *(jax.ShapeDtypeStruct(s.shape, F32) for s in shapes[1:])),
        in_specs=[vmem] * 4,
        out_specs=(smem, vmem, vmem, vmem),
        name="hand_out",
    )(*shapes)
    return loss.reshape(()), grad_in, grad_out.T, grad_features.reshape(1, OWN * TILE, TILE)


def solution(mesh):
    placed = (
        P("col", "row", None),
        P("row", "col", None, None, None),
        P("row", "col", None),
        P("row", "col", None),
        P("row", "col"),
        P(),
        P(),
        P("row", "col"),
        P("row", "col"),
    )
    return jax.shard_map(
        shards,
        mesh=mesh,
        in_specs=placed,
        out_specs=(P(), P(), P(), P("col", "row", None)),
        check_vma=False,
    )
```

```python
import jax
import jax.numpy as jnp
from jax import lax
from jax.experimental import pallas as pl
from jax.experimental.pallas import tpu as pltpu
from jax.sharding import PartitionSpec as P

F32, BF16, I32 = jnp.float32, jnp.bfloat16, jnp.int32
TILE = 128
CHUNKS = ((0, 64), (64, 64))
SLOTS = 96
ROW_TILES = 96
COL_TILES = 48
OWN = 6
HALF = 3
CLS = 172
CLS_ROWS = 176
HID = 256
UNROLL = 48
N_SEMS = 86
WIDER2 = (True, False)
WIDER4 = (True, True)
FAR_PAIR, SIDE_UP, SIDE_DOWN, FREE, FAR, LATE, NEAR = range(7)
FORWARD = (
    ("gather", 0, "own"), ("gather", 1, "own"), ("gather", 0, "far"), ("slots", 0, ""),
    ("weights", 0, ""), ("gather", 1, "far"), ("gather", 0, "beside"), ("turn", 0, ""),
    ("gather", 0, "last"), ("count", 0, ""), ("gather", 1, "beside"), ("gather", 1, "last"),
    ("gather", 0, "done"), ("products", 0, ""), ("count", 1, ""), ("cores", 0, ""),
    ("gather", 1, "done"), ("products", 1, ""), ("scatter", 0, "start"), ("cores", 1, ""),
    ("scatter", 1, "start"), ("count", 2, ""), ("scatter", 0, "far"), ("scatter", 0, "near"),
    ("count", 3, ""), ("scatter", 1, "far"), ("scatter", 1, "near"), ("scatter", 0, "late"),
    ("scatter", 1, "late"), ("scatter", 0, "done"), ("scatter", 1, "done"),
)
BACKWARD = (
    ("gather", 0, "own"), ("gather", 1, "own"), ("small", 0, ""), ("gather", 0, "far"),
    ("gather", 1, "far"), ("gather", 0, "beside"), ("gather", 0, "last"), ("small", 1, ""),
    ("gather", 1, "beside"), ("gather", 1, "last"), ("small", 2, ""), ("gather", 0, "done"),
    ("handed", 0, ""), ("products", 0, ""), ("scatter", 0, "start"), ("gather", 1, "done"),
    ("small", 3, ""), ("handed", 1, ""), ("products", 1, ""), ("small", 4, ""),
    ("scatter", 0, "far"), ("scatter", 1, "start"), ("scatter", 0, "near"), ("scatter", 1, "far"),
    ("small", 5, ""), ("scatter", 1, "near"), ("scatter", 0, "late"), ("scatter", 1, "late"),
    ("scatter", 0, "done"), ("scatter", 1, "done"),
)
NT = (((1,), (1,)), ((), ()))


def gather(copy, counter, buf, block, ring, pair, landed):
    def expect(blocks):
        return counter(buf.at[0 : blocks * OWN])

    def send(dr, dp, half, to, recv):
        at = buf.at[pl.ds(block(dr, dp) * OWN + half * HALF, HALF)]
        copy(at, at, to, sent, recv)

    up, down, across = ring(1), ring(-1), pair
    sent, first, beside, far, rest = expect(7), expect(1), expect(1), expect(1), expect(4)
    send(0, 0, 0, up, first)
    send(0, 0, 1, down, first)
    send(0, 0, 0, across, beside)
    send(0, 0, 1, up, rest)
    send(0, 0, 0, down, rest)
    send(0, 0, 1, across, beside)
    yield "own"
    first.wait()
    send(-1, 0, 0, up, far)
    send(1, 0, 1, down, far)
    landed(-1, 0, 0)
    landed(1, 0, 1)
    yield "far"
    beside.wait()
    for half in (0, 1):
        send(0, 1, half, up, rest)
        send(0, 1, half, down, rest)
    landed(0, 1)
    yield "beside"
    far.wait()
    send(2, 0, 0, across, rest)
    send(2, 0, 1, across, rest)
    landed(2, 0)
    yield "last"
    rest.wait()
    landed(-1, 0, 1)
    landed(1, 0, 0)
    landed(-1, 1)
    landed(1, 1)
    landed(2, 1)
    yield "done"


def scatter(copy, counter, out, inn, out_near, in_near, ring, pair, source, result):
    up, down, across = ring(1), ring(-1), pair
    both = (0, OWN)
    low, high = (0, HALF), (HALF, OWN)

    def fill(ref, span, chip, *received):
        local = source(*chip)
        for t in range(*span):
            value = local(t)
            for n in received:
                value = value + inn[n, t].astype(F32)
            ref[t] = value.astype(ref.dtype)

    def send(slot, span, to, recv):
        at = pl.ds(span[0], span[1] - span[0])
        copy(out.at[slot, at], inn.at[slot, at], to, sent, recv)

    sent, sent_near = counter(out.at[0:NEAR]), counter(out_near)
    far_pair = [counter(inn.at[FAR_PAIR, a:b]) for a, b in (low, high)]
    side, free, far, late = counter(inn.at[0:2]), counter(inn.at[0]), counter(inn.at[0]), counter(inn.at[0])
    near = counter(in_near)
    for n, span in enumerate((low, high)):
        fill(out.at[FAR_PAIR], span, (2, 1))
        send(FAR_PAIR, span, across, far_pair[n])
    fill(out.at[SIDE_UP], both, (1, 1))
    send(SIDE_UP, both, up, side)
    fill(out.at[SIDE_DOWN], both, (-1, 1))
    send(SIDE_DOWN, both, down, side)
    fill(out.at[FREE], high, (1, 0))
    send(FREE, high, up, free)
    fill(out.at[FREE], low, (-1, 0))
    send(FREE, low, down, free)
    yield "start"
    far_pair[0].wait()
    fill(out.at[FAR], low, (2, 0), FAR_PAIR)
    send(FAR, low, up, far)
    far_pair[1].wait()
    fill(out.at[FAR], high, (2, 0), FAR_PAIR)
    send(FAR, high, down, far)
    yield "far"
    side.wait()
    for a, b in (low, high):
        fill(out_near, (a, b), (0, 1), SIDE_UP, SIDE_DOWN)
        copy(out_near.at[a:b], in_near.at[a:b], across, sent_near, near)
    yield "near"
    far.wait()
    fill(out.at[LATE], low, (1, 0), FAR)
    send(LATE, low, up, late)
    fill(out.at[LATE], high, (-1, 0), FAR)
    send(LATE, high, down, late)
    yield "late"
    free.wait()
    near.wait()
    late.wait()
    local = source(0, 0)
    for t in range(OWN):
        value = local(t) + inn[FREE, t].astype(F32) + inn[LATE, t].astype(F32)
        result(t, value + in_near[t].astype(F32))
    yield "done"


def order_slots(key, other, live, slots, tiles, idx, base):
    sub = lax.broadcasted_iota(I32, (slots, slots), 0)
    lane = lax.broadcasted_iota(I32, (slots, slots), 1)
    diag = sub == lane

    def column(v):
        return jnp.sum(jnp.where(diag, jnp.broadcast_to(v, (slots, slots)), 0), axis=1, keepdims=True)

    lane1 = lax.broadcasted_iota(I32, (1, slots), 1)
    sort_l = jnp.where(live > 0, key * TILE + lane1, tiles * TILE + lane1)
    sort_c, key_c, other_c, live_c = column(sort_l), column(key), column(other), column(live)
    rank_c = jnp.sum((jnp.broadcast_to(sort_l, (slots, slots)) < sort_c).astype(I32), axis=1, keepdims=True)

    def place(v):
        return jnp.sum(jnp.where(rank_c == lane, v, 0), axis=0, keepdims=True)

    idx[base : base + 1, 0:slots] = place(sub)
    idx[base + 1 : base + 2, 0:slots] = place(other_c)
    idx[base + 2 : base + 3, 0:slots] = place(key_c)
    below = jnp.sum(jnp.where(key_c <= lane, live_c, 0), axis=0, keepdims=True)
    same = jnp.sum(jnp.where(key_c == lane, live_c, 0), axis=0, keepdims=True)
    idx[base + 3 : base + 4, 0:slots] = jnp.maximum(below - 1, 0)
    idx[base + 4 : base + 5, 0:slots] = same


def tile_products(product, sums, where, base):
    def step(i, acc):
        for u in range(UNROLL):
            k = i * UNROLL + u
            prod = product(where[base, k], where[base + 1, k])
            keep = where[base + 2, k] == where[base + 2, jnp.maximum(k - 1, 0)]
            acc = jnp.where(keep, acc, 0.0) + prod
            sums[k] = acc
        return acc

    lax.fori_loop(0, SLOTS // UNROLL, step, jnp.zeros(sums.shape[1:], F32))


class Counter:
    def __init__(self, sem, like):
        self.sem, self.like = sem, like
        self.waiting = True

    def wait(self):
        if self.waiting:
            self.waiting = False
            pltpu.make_async_copy(self.like, self.like, self.sem).wait()


def run_to(phase, step):
    while next(phase) != step:
        pass


def kernel(
    feat, vals_hbm, trow_h, tcol_h, tcnt_h, win_h, wout_h, lab_h, msk_h,
    loss_o, gin_o, gout_o, gf_o,
    trow, tcol, tcnt, win, wout, lab, msk,
    feat_v, vals, vals_t, gf_t,
    idx, where, win_t, wpad, wpad_t, rows_s, hid_s, lgrad_s, pre_s, gin_s, gout_s,
    m_part, y_in, m_y, x_in, z_all, c_out, c_in, final,
    cnt_out, cnt_in, sems, local_sem, *parts,
):
    row, col = lax.axis_index("row"), lax.axis_index("col")
    zl, y = row // 4, row % 4
    zh, x, k = col // 8, (col // 2) % 4, col % 2
    count = len(CHUNKS)
    xt, gt, sums, core_out, core_in = (parts[n * count : (n + 1) * count] for n in range(5))
    out2, in2, out4, in4, near_out2, near_in2, near_out4, near_in4 = (
        parts[n * count : (n + 1) * count] for n in range(5, 13)
    )

    def chip(zl_=zl, y_=y, zh_=zh, x_=x, k_=k):
        return {"row": zl_ * 4 + y_, "col": (zh_ * 4 + x_) * 2 + k_}

    def y_at(d):
        return chip(y_=(y + d + 4) % 4)

    def x_at(d):
        return chip(x_=(x + d + 4) % 4)

    def row_chip(dr, dp):
        return (zl + dp) % 2 * 4 + (y + dr + 4) % 4

    def col_chip(dr, dp):
        return (zh + dp) % 2 * 4 + (x + dr + 4) % 4

    z_others = [chip(zl_=1 - zl), chip(zh_=1 - zh), chip(zl_=1 - zl, zh_=1 - zh)]
    y_others = [y_at(d) for d in (1, 2, 3)]
    x_others = [x_at(d) for d in (1, 2, 3)]
    y_pair, x_pair, core = chip(zl_=1 - zl), chip(zh_=1 - zh), chip(k_=1 - k)

    counters = []

    def counter(like):
        counters.append(Counter(sems.at[len(counters)], like))
        return counters[-1]

    def copy(src, dst, to, send, recv):
        pltpu.make_async_remote_copy(
            src_ref=src, dst_ref=dst, send_sem=send.sem, recv_sem=recv.sem,
            device_id=to, device_id_type=pl.DeviceIdType.MESH,
        ).start()

    load_own = pltpu.make_async_copy(feat, feat_v, local_sem.at[0])
    load_own.start()
    load_vals = pltpu.make_async_copy(vals_hbm.at[0, 0], vals, local_sem.at[1])
    load_vals.start()
    pairs = ((trow_h, trow), (tcol_h, tcol), (tcnt_h, tcnt), (win_h, win), (wout_h, wout), (lab_h, lab), (msk_h, msk))
    loads = [pltpu.make_async_copy(src, dst, local_sem.at[3 + n]) for n, (src, dst) in enumerate(pairs)]
    for c in loads:
        c.start()

    partners = [*y_others, *x_others, *z_others, core]
    barrier = pltpu.get_barrier_semaphore()
    for p in partners:
        pl.semaphore_signal(barrier, inc=1, device_id=p, device_id_type=pl.DeviceIdType.MESH)
    load_own.wait()
    for t in range(OWN):
        turned = feat_v[t].astype(F32).T.astype(BF16)
        for c, (first, width) in enumerate(CHUNKS):
            xt[c][row * OWN + t] = turned[first : first + width]
    pl.semaphore_wait(barrier, len(partners))

    count_groups = [y_others, x_others, z_others, [core]]
    count_copies = []

    def count_send(stage):
        group = count_groups[stage]
        like = cnt_in.at[stage, 0 : len(group)]
        send, recv = counter(like), counter(like)
        for n, to in enumerate(group):
            copy(cnt_out.at[stage], cnt_in.at[stage, n], to, send, recv)
        count_copies.append(recv)

    def count_take(stage):
        count_copies[stage].wait()
        value = cnt_out[stage]
        for n in range(len(count_groups[stage])):
            value = value + cnt_in[stage, n]
        cnt_out[stage + 1] = value

    def prepare_slots():
        slot = lax.broadcasted_iota(I32, (1, SLOTS), 1)
        live = (slot < tcnt[...]).astype(I32)
        idx[...] = jnp.zeros(idx.shape, I32)
        order_slots(trow[...], tcol[...], live, SLOTS, ROW_TILES, idx, 0)
        order_slots(tcol[...], trow[...], live, SLOTS, ROW_TILES, idx, 5)
        to_smem = pltpu.make_async_copy(idx, where, local_sem.at[2])
        to_smem.start()
        to_smem.wait()

    def prepare_weights():
        win_t[...] = win[...].astype(F32).T.astype(BF16)
        wpad[...] = jnp.zeros(wpad.shape, BF16)
        wpad[0:CLS] = wout[...]
        wpad_t[...] = wpad[...].astype(F32).T.astype(BF16)
        lgrad_s[...] = jnp.zeros(lgrad_s.shape, BF16)

    def row_sum(chunk, tile):
        return sums[chunk][where[3, tile]] * (where[4, tile] > 0).astype(F32)

    def col_sum(chunk, tile):
        return sums[chunk][where[8, tile]] * (where[9, tile] > 0).astype(F32)

    def forward(chunk):
        def product(slot, other):
            return jnp.dot(xt[chunk][other], vals_t[slot], preferred_element_type=F32)

        tile_products(product, sums[chunk], where, 0)

    def backward(chunk):
        def product(slot, other):
            return jnp.dot(gt[chunk][other], vals[slot], preferred_element_type=F32)

        tile_products(product, sums[chunk], where, 5)

    classes = [(2, 1), (1, 1), (-1, 1), (1, 0), (-1, 0), (2, 0), (0, 1), (0, 0)]
    core_first, core_rest = {}, {}

    def core_send(chunk):
        send = counter(core_out[chunk])
        core_first[chunk], core_rest[chunk] = counter(core_in[chunk].at[0]), counter(core_in[chunk].at[1:8])
        for n, (dr, dp) in enumerate(classes):
            base = (col_chip(dr, dp) * 2 + 1 - k) * OWN
            for t in range(OWN):
                core_out[chunk][n, t] = row_sum(chunk, base + t)
            recv = core_rest[chunk] if n else core_first[chunk]
            copy(core_out[chunk].at[n], core_in[chunk].at[n], core, send, recv)

    def forward_source(chunk):
        def source(dr, dp):
            base, n = (col_chip(dr, dp) * 2 + k) * OWN, classes.index((dr, dp))
            (core_rest if n else core_first)[chunk].wait()
            return lambda t: row_sum(chunk, base + t) + core_in[chunk][n, t]

        return source

    def take_rows(chunk):
        first, width = CHUNKS[chunk]

        def result(t, value):
            lanes = slice(t % 2 * TILE, t % 2 * TILE + TILE)
            rows_s[t // 2, first : first + width, lanes] = value.astype(BF16)

        return result

    def turn_tiles():
        load_vals.wait()

        @pl.loop(0, SLOTS, unroll=8)
        def _(n):
            vals_t[n] = vals[n].T

    def count_step(stage):
        if stage == 0:
            cnt_out[0] = jnp.broadcast_to(jnp.sum(msk[...].astype(F32), axis=1, keepdims=True), (8, TILE))
        else:
            count_take(stage - 1)
        count_send(stage)

    gathers = [gather(copy, counter, xt[c], row_chip, y_at, y_pair, lambda *chip: None) for c in range(count)]
    scatters = [
        scatter(copy, counter, out2[c], in2[c], near_out2[c], near_in2[c], x_at, x_pair, forward_source(c), take_rows(c)) for c in range(count)
    ]
    loaded = False
    for what, c, step in FORWARD:
        if what in ("count", "slots", "weights") and not loaded:
            loaded = True
            for load in loads:
                load.wait()
        if what == "gather":
            run_to(gathers[c], step)
        elif what == "scatter":
            run_to(scatters[c], step)
        elif what == "products":
            forward(c)
        elif what == "cores":
            core_send(c)
        elif what == "count":
            count_step(c)
        elif what == "slots":
            prepare_slots()
        elif what == "weights":
            prepare_weights()
        elif what == "turn":
            turn_tiles()
    count_take(3)

    counted = cnt_out[4][0:1, 0:1]
    sub = lax.broadcasted_iota(I32, (CLS_ROWS, 2 * TILE), 0)
    loss = jnp.zeros((1, 2 * TILE), F32)
    for j in range(OWN // 2):
        nodes = slice(j * 2 * TILE, (j + 1) * 2 * TILE)
        pre = jnp.dot(win_t[...], rows_s[j], preferred_element_type=F32)
        sig = jax.nn.sigmoid(pre)
        hidden = (pre * sig).astype(BF16)
        hid_s[j] = hidden
        logits = jnp.dot(wpad[0:CLS_ROWS], hidden, preferred_element_type=F32)
        log_norm = jnp.log(jnp.sum(jnp.where(sub < CLS, jnp.exp(logits), 0.0), axis=0, keepdims=True))
        onehot = (sub == lab[:, nodes]).astype(F32)
        weight = msk[:, nodes].astype(F32)
        loss = loss + weight * (log_norm - jnp.sum(logits * onehot, axis=0, keepdims=True))
        prob = jnp.where(sub < CLS, jnp.exp(logits - log_norm), 0.0)
        lgrad_s[j, 0:CLS_ROWS] = ((weight / counted) * (prob - onehot)).astype(BF16)
        back = jnp.dot(wpad_t[...], lgrad_s[j], preferred_element_type=F32)
        grad_pre = (back * sig * (1.0 + pre * (1.0 - sig))).astype(BF16)
        pre_s[j] = grad_pre
        feed = jnp.dot(win[...], grad_pre, preferred_element_type=F32).astype(BF16)
        for c, (first, width) in enumerate(CHUNKS):
            for u in (0, 1):
                gt[c][col * OWN + 2 * j + u] = feed[first : first + width, u * TILE : (u + 1) * TILE]
    loss = jnp.sum(loss, axis=1, keepdims=True) / counted

    steps = {}

    def spread(name, like, moves):
        send, steps[name] = counter(like), counter(like)
        for src, dst, to in moves:
            copy(src, dst, to, send, steps[name])

    def weight_grads():
        gin_s[...] = jnp.zeros((TILE, HID), F32)
        gout_s[...] = jnp.zeros((HID, HID), F32)

        @pl.loop(0, OWN // 2)
        def _(j):
            gin_s[...] += lax.dot_general(rows_s[j], pre_s[j], NT, preferred_element_type=F32)
            gout_s[...] += lax.dot_general(lgrad_s[j], hid_s[j], NT, preferred_element_type=F32)

        sub = lax.broadcasted_iota(I32, (8, HID), 0)
        lane = lax.broadcasted_iota(I32, (8, HID), 1)
        tail = gout_s[HID - 8 : HID]
        gout_s[HID - 8 : HID] = jnp.where((sub == 7) & (lane == 0), jnp.broadcast_to(loss, (8, HID)), tail)
        for n in range(16):
            for r in range(0, 24, 8):
                at = n * 24 + r
                piece = gin_s[at : at + 8] if at < TILE else gout_s[at - TILE : at - TILE + 8]
                m_part[n // 4, n % 4, r : r + 8] = piece
        spread("y", y_in, [(m_part.at[(y + d) % 4], y_in.at[d - 1], to) for d, to in zip((1, 2, 3), y_others)])

    def sum_y():
        steps["y"].wait()
        for n in range(4):
            m_y[n] = m_part[y, n] + y_in[0, n] + y_in[1, n] + y_in[2, n]
        spread("x", x_in, [(m_y.at[(x + d) % 4], x_in.at[d - 1], to) for d, to in zip((1, 2, 3), x_others)])

    def sum_x():
        steps["x"].wait()
        me = zh * 2 + zl
        z_all[me] = m_y[x] + x_in[0] + x_in[1] + x_in[2]
        spread("z", z_all.at[0:3], [(z_all.at[me], z_all.at[me], to) for to in z_others])

    def sum_z():
        steps["z"].wait()
        c_out[...] = (z_all[0] + z_all[1]) + (z_all[2] + z_all[3])
        spread("core", c_in, [(c_out, c_in, core)])

    def sum_core():
        steps["core"].wait()
        final[x, y] = c_out[...] + c_in[...]
        spread("spread_y", final.at[0, 0:3], [(final.at[x, y], final.at[x, y], to) for to in y_others])

    def spread_x():
        steps["spread_y"].wait()
        spread("spread_x", final.at[0:3], [(final.at[x], final.at[x], to) for to in x_others])

    handed = [(counter(gt[c].at[0 : 8 * OWN]), counter(gt[c].at[0 : 8 * OWN])) for c in range(count)]

    def hand(chunk):
        def landed(dr, dp, half=None):
            first, size = (0, OWN) if half is None else (half * HALF, HALF)
            at = gt[chunk].at[pl.ds((col_chip(dr, dp) * 2 + k) * OWN + first, size)]
            copy(at, at, core, *handed[chunk])

        return landed

    def take_grads(chunk):
        first, width = CHUNKS[chunk]

        def result(t, value):
            gf_t[t, first : first + width] = value

        return result

    def backward_source(chunk):
        def source(dr, dp):
            base = row_chip(dr, dp) * OWN
            return lambda t: col_sum(chunk, base + t)

        return source

    gathers = [
        gather(copy, counter, gt[c], lambda dr, dp: col_chip(dr, dp) * 2 + k, x_at, x_pair, hand(c)) for c in range(count)
    ]
    scatters = [
        scatter(copy, counter, out4[c], in4[c], near_out4[c], near_in4[c], y_at, y_pair, backward_source(c), take_grads(c)) for c in range(count)
    ]
    small = (weight_grads, sum_y, sum_x, sum_z, sum_core, spread_x)
    for what, c, step in BACKWARD:
        if what == "gather":
            run_to(gathers[c], step)
            if step == "own":
                hand(c)(0, 0)
        elif what == "scatter":
            run_to(scatters[c], step)
        elif what == "handed":
            handed[c][1].wait()
        elif what == "products":
            backward(c)
        elif what == "small":
            small[c]()
    for t in range(OWN):
        gf_o[t] = gf_t[t].T

    steps["spread_x"].wait()
    for n in range(16):
        for r in range(0, 24, 8):
            at = n * 24 + r
            piece = final[n % 4, n // 4, r : r + 8]
            if at < TILE:
                gin_o[at : at + 8] = piece
            else:
                put = min(8, CLS - (at - TILE))
                if put > 0:
                    gout_o[at - TILE : at - TILE + put] = piece[0:put]
                if at == TILE + HID - 8:
                    loss_o[...] = jnp.broadcast_to(piece[7:8, 0:1], loss_o.shape)

    for c in counters:
        c.wait()


def hand_out(loss, gin, gout, gf, loss_o, gin_o, gout_o, gf_o):
    loss_o[0] = loss[0, 0]
    gin_o[...] = gin[...]
    gout_o[...] = gout[...]
    gf_o[...] = gf[...]


def shards(
    features,
    tile_values,
    tile_rows,
    tile_cols,
    tile_counts,
    in_weight,
    out_weight,
    labels,
    loss_mask,
):
    vmem = pl.BlockSpec(memory_space=pltpu.VMEM)
    smem = pl.BlockSpec(memory_space=pltpu.SMEM)
    hbm = pl.BlockSpec(memory_space=pl.ANY)
    block = (OWN, TILE, TILE)
    loss, grad_in, grad_out, grad_features = pl.pallas_call(
        kernel,
        out_shape=(
            pltpu.VMEM((8, TILE), F32),
            pltpu.VMEM((TILE, HID), F32),
            pltpu.VMEM((CLS, HID), F32),
            pltpu.VMEM(block, F32),
        ),
        in_specs=[hbm] * 9,
        out_specs=(vmem, vmem, vmem, vmem),
        scratch_shapes=[
            pltpu.VMEM((1, SLOTS), I32),
            pltpu.VMEM((1, SLOTS), I32),
            pltpu.VMEM((1, 1), I32),
            pltpu.VMEM((TILE, HID), BF16),
            pltpu.VMEM((CLS, HID), BF16),
            pltpu.VMEM((1, OWN * TILE), I32),
            pltpu.VMEM((1, OWN * TILE), I32),
            pltpu.VMEM(block, BF16),
            pltpu.VMEM((SLOTS, TILE, TILE), BF16),
            pltpu.VMEM((SLOTS, TILE, TILE), BF16),
            pltpu.VMEM(block, F32),
            pltpu.VMEM((16, TILE), I32),
            pltpu.SMEM((16, TILE), I32),
            pltpu.VMEM((HID, TILE), BF16),
            pltpu.VMEM((HID, HID), BF16),
            pltpu.VMEM((HID, HID), BF16),
            pltpu.VMEM((OWN // 2, TILE, 2 * TILE), BF16),
            pltpu.VMEM((OWN // 2, HID, 2 * TILE), BF16),
            pltpu.VMEM((OWN // 2, HID, 2 * TILE), BF16),
            pltpu.VMEM((OWN // 2, HID, 2 * TILE), BF16),
            pltpu.VMEM((TILE, HID), F32),
            pltpu.VMEM((HID, HID), F32),
            pltpu.VMEM((4, 4, 24, HID), F32),
            pltpu.VMEM((3, 4, 24, HID), F32),
            pltpu.VMEM((4, 24, HID), F32),
            pltpu.VMEM((3, 24, HID), F32),
            pltpu.VMEM((4, 24, HID), F32),
            pltpu.VMEM((24, HID), F32),
            pltpu.VMEM((24, HID), F32),
            pltpu.VMEM((4, 4, 24, HID), F32),
            pltpu.VMEM((5, 8, TILE), F32),
            pltpu.VMEM((4, 3, 8, TILE), F32),
            pltpu.SemaphoreType.DMA((N_SEMS,)),
            pltpu.SemaphoreType.DMA((10,)),
            *(pltpu.VMEM((COL_TILES, width, TILE), BF16) for _, width in CHUNKS),
            *(pltpu.VMEM((ROW_TILES, width, TILE), BF16) for _, width in CHUNKS),
            *(pltpu.VMEM((SLOTS, width, TILE), F32) for _, width in CHUNKS),
            *(pltpu.VMEM((8, OWN, width, TILE), F32) for _, width in CHUNKS),
            *(pltpu.VMEM((8, OWN, width, TILE), F32) for _, width in CHUNKS),
            *(pltpu.VMEM((NEAR, OWN, width, TILE), BF16) for _ in range(4) for _, width in CHUNKS),
            *(
                pltpu.VMEM((OWN, width, TILE), F32 if wider[c] else BF16)
                for wider in (WIDER2, WIDER2, WIDER4, WIDER4)
                for c, (_, width) in enumerate(CHUNKS)
            ),
        ],
        compiler_params=pltpu.CompilerParams(
            collective_id=0, has_side_effects=True, vmem_limit_bytes=56 * 1024 * 1024
        ),
        name="graph_layer",
    )(
        features.reshape(OWN, TILE, TILE),
        tile_values,
        tile_rows[0],
        tile_cols[0],
        tile_counts,
        in_weight,
        out_weight.T,
        labels,
        loss_mask,
    )
    shapes = [pltpu.with_memory_space_constraint(v, pltpu.VMEM) for v in (loss, grad_in, grad_out, grad_features)]
    loss, grad_in, grad_out, grad_features = pl.pallas_call(
        hand_out,
        out_shape=(jax.ShapeDtypeStruct((1,), F32), *(jax.ShapeDtypeStruct(s.shape, F32) for s in shapes[1:])),
        in_specs=[vmem] * 4,
        out_specs=(smem, vmem, vmem, vmem),
        name="hand_out",
    )(*shapes)
    return loss.reshape(()), grad_in, grad_out.T, grad_features.reshape(1, OWN * TILE, TILE)


def solution(mesh):
    placed = (
        P("col", "row", None),
        P("row", "col", None, None, None),
        P("row", "col", None),
        P("row", "col", None),
        P("row", "col"),
        P(),
        P(),
        P("row", "col"),
        P("row", "col"),
    )
    return jax.shard_map(
        shards,
        mesh=mesh,
        in_specs=placed,
        out_specs=(P(), P(), P(), P("col", "row", None)),
        check_vma=False,
    )
```
